32 devices in a mesh: fil: 8 (over z, x), row: 4 (over y, core).
Axes of the slice: x: 2, y: 2, z: 4, core: 2. Of those that a mesh axis runs over, the one named last changes fastest.
Arguments:
- images: bfloat16 [64, 2, 256, 128], P('fil', None, 'row'), may hold values from -6 to 6
- defocus: float32 [64], P('fil'), may hold values from 0.5 to 2
- references: bfloat16 [8, 2, 256, 128], P('fil', None, 'row'), may hold values from -0.0234375 to 0.0234375
- offsets: int32 [64, 32, 2], P('fil'), may hold values from -8 to 8
- posterior: int32 [64, 32], P('fil'), may hold values from 0 to 255
- class_ids: int32 [64], P('fil'), may hold values from 0 to 15
- seg_count: int32 [8], P('fil'), may hold values from 1 to 8, as said below
Outputs:
- scores: float32 [64, 32, 8], P('fil', 'row')
- averages: float32 [16, 65536], P(None, ('row', 'fil'))
The draws below stay inside these ranges and needn't reach their ends.
Inputs may be any that keep to these rules, and one draw needn't show every extreme that they name: `seg_count`: each filament has its segments in the first slots of its 8; some filament has exactly 8.
All inputs are finite; a program needn't handle non-finite values.
Results may differ from the reference program's by a relative error of at most 0.0029.
Values may be sent and summed in bfloat16 or wider, within the bound.
A program may use at most 128 MiB of HBM per device.

```python
import math
import jax
import jax.numpy as jnp
from jax import lax

FROWS = 256
FCOLS = 128
SHIFTS = 32
CLASSES = 16
SEG_FIL = 8
FILS = 8
SEGS = 64
REFS = 8


def draw_seg_count(key, part):
    first = jax.random.fold_in(key, 11)
    second = jax.random.fold_in(key, 23)
    counts = jax.random.randint(first, (FILS,), 1, SEG_FIL + 1, dtype=jnp.int32)
    spot = jax.random.randint(second, (), 0, FILS, dtype=jnp.int32)
    return jnp.where(jnp.arange(FILS, dtype=jnp.int32) == spot, SEG_FIL, counts).astype(jnp.int32)


def place_ends(array, rng, least, largest):
    dims = array.shape
    index_at = [jax.random.randint(jax.random.fold_in(rng, axis), (), 0, dims[axis]) for axis in range(len(dims))]
    array = array.at[tuple(index_at)].set(least)
    longest = dims.index(max(dims))
    index_at[longest] = (index_at[longest] + 1) % dims[longest]
    return array.at[tuple(index_at)].set(largest)


def shard_levels(key, shape, shards, low, high):
    level, own = 1.0, jax.random.fold_in(key, 6)
    for dim, parts in shards:
        draws = jnp.exp(jax.random.uniform(jax.random.fold_in(own, dim), (parts,), jnp.float32, low / len(shards), high / len(shards)))
        level = level * jnp.repeat(draws, shape[dim] // parts).reshape([-1 if axis == dim else 1 for axis in range(len(shape))])
    return level


def bell_draw(own_key, shape, deviation, bound, pieces=(), held_as=jnp.bfloat16):
    factor_of = shard_levels(own_key, shape, pieces, -0.22, 0.18) if pieces else 1.0
    array = jax.random.normal(own_key, shape, jnp.float32) * deviation * factor_of
    return jnp.minimum(jnp.maximum(array, -bound), bound).astype(held_as)


def setup_inputs(seed: int = 0) -> dict:
    streams_of = jax.random.split(jax.random.key(seed), 8)
    return {
        "images": bell_draw(streams_of[0], (SEGS, 2, FROWS, FCOLS), 1.0, 6.0, ((0, 8), (2, 4))),
        "defocus": jnp.clip(jnp.exp(math.log(2.0) - 1.3862944 * jax.random.uniform(streams_of[1], (SEGS,), jnp.float32) ** shard_levels(streams_of[1], (SEGS,), ((0, 8),), -0.2, 0.2)), 0.5, 2.0),
        "references": bell_draw(streams_of[2], (REFS, 2, FROWS, FCOLS), (2 * FROWS * FCOLS) ** -0.5, 0.0234375, ((0, 8), (2, 4))),
        "offsets": place_ends(jax.random.randint(streams_of[3], (SEGS, SHIFTS, 2), -8, 9), jax.random.fold_in(streams_of[3], 1), -8, 8).astype(jnp.int32),
        "posterior": place_ends(jax.random.randint(streams_of[4], (SEGS, SHIFTS), 0, 256), jax.random.fold_in(streams_of[4], 1), 0, 255).astype(jnp.int32),
        "class_ids": place_ends(jax.random.randint(streams_of[5], (SEGS,), 0, CLASSES), jax.random.fold_in(streams_of[5], 1), 0, CLASSES - 1).astype(jnp.int32),
        "seg_count": draw_seg_count(jax.random.fold_in(streams_of[7], 71), 0),
    }


def wave_tables(shift_rows, shift_cols, row_freq, col_freq, box):
    row_angle = (shift_rows[..., None] * row_freq % box).astype(jnp.float32) * (-2.0 * math.pi / box)
    col_angle = (shift_cols[..., None] * col_freq % box).astype(jnp.float32) * (-2.0 * math.pi / box)
    row_cos = jnp.cos(row_angle)[..., :, None]
    row_sin = jnp.sin(row_angle)[..., :, None]
    col_cos = jnp.cos(col_angle)[..., None, :]
    col_sin = jnp.sin(col_angle)[..., None, :]
    phase_re = row_cos * col_cos - row_sin * col_sin
    phase_im = row_cos * col_sin + row_sin * col_cos
    return (phase_re, phase_im)

def contrast(defocus_vals, row_freq, col_freq, box):
    radius = (row_freq[:, None] * row_freq[:, None] + col_freq[None, :] * col_freq[None, :]).astype(jnp.float32) / float(box * box)
    return -jnp.sin(200.0 * defocus_vals[:, None, None] * radius[None] + 0.1)

def aligned_rows(block_images, gain, block_offsets, row_freq, col_freq, box):
    phase_re, phase_im = wave_tables(block_offsets[..., 0], block_offsets[..., 1], row_freq, col_freq, box)
    scaled = gain[:, None]
    real_part = block_images[:, 0].astype(jnp.float32)[:, None]
    imag_part = block_images[:, 1].astype(jnp.float32)[:, None]
    aligned_re = scaled * (real_part * phase_re - imag_part * phase_im)
    aligned_im = scaled * (real_part * phase_im + imag_part * phase_re)
    stacked = jnp.stack([aligned_re, aligned_im], axis=3).astype(jnp.bfloat16)
    return stacked.reshape(stacked.shape[0] * stacked.shape[1], -1)

def reference(images, defocus, references, offsets, posterior, class_ids, seg_count):
    segs = images.shape[0]
    box = FROWS
    rows = images.shape[2]
    cols = images.shape[3]
    row_freq = (jnp.arange(rows, dtype=jnp.int32) + box // 2) % box - box // 2
    col_freq = jnp.arange(cols, dtype=jnp.int32)
    live = (jnp.arange(SEG_FIL, dtype=jnp.int32)[None, :] < seg_count[:, None]).reshape(-1).astype(jnp.float32)
    weight = live[:, None] * posterior.astype(jnp.float32) / 256.0
    panel = jnp.transpose(references, (0, 2, 1, 3)).reshape(references.shape[0], -1)
    classes = jnp.arange(CLASSES, dtype=jnp.int32)
    blocks = segs // 8

    def step(carry, inputs):
        numer, denom = carry
        block_images, block_defocus, block_offsets, block_weight, block_live, block_ids = inputs
        ctf = contrast(block_defocus, row_freq, col_freq, box)
        aligned = aligned_rows(block_images, ctf * block_live[:, None, None], block_offsets, row_freq, col_freq, box)
        block_scores = lax.dot_general(aligned, panel, (((1,), (1,)), ((), ())), preferred_element_type=jnp.float32)
        member = (block_ids[None, :] == classes[:, None]).astype(jnp.float32)
        spread = (member[:, :, None] * block_weight[None]).astype(jnp.bfloat16).reshape(CLASSES, -1)
        numer = numer + jnp.dot(spread, aligned, preferred_element_type=jnp.float32)
        totals = member * lax.optimization_barrier(jnp.sum(block_weight, axis=1))[None, :]
        denom = denom + jnp.dot(totals, (ctf * ctf).reshape(ctf.shape[0], -1), precision=lax.Precision.HIGHEST, preferred_element_type=jnp.float32)
        return ((numer, denom), block_scores.reshape(8, SHIFTS, -1))
    inputs = (images.reshape(blocks, 8, 2, rows, cols), defocus.reshape(blocks, 8), offsets.reshape(blocks, 8, SHIFTS, 2), weight.reshape(blocks, 8, SHIFTS), live.reshape(blocks, 8), class_ids.reshape(blocks, 8))
    start = (jnp.zeros((CLASSES, rows * 2 * cols), jnp.float32), jnp.zeros((CLASSES, rows * cols), jnp.float32))
    (numer, denom), scores = lax.scan(step, start, inputs)
    wide = jnp.broadcast_to(denom.reshape(CLASSES, rows, 1, cols), (CLASSES, rows, 2, cols)).reshape(CLASSES, -1)
    averages = numer * lax.rsqrt(wide + 1.0)
    return (scores.reshape(segs, SHIFTS, -1), averages)
```

```python
import math

import jax
import jax.numpy as jnp
from jax import lax
from jax.experimental import pallas as pl
from jax.experimental.pallas import tpu as pltpu
from jax.sharding import PartitionSpec as P

MESH = pl.DeviceIdType.MESH

FROWS = 256
SHIFTS = 32
CLASSES = 16
SEG_FIL = 8


def wave_tables(shift_rows, shift_cols, row_freq, col_freq, box):
    row_angle = (shift_rows[..., None] * row_freq % box).astype(jnp.float32) * (
        -2.0 * math.pi / box
    )
    col_angle = (shift_cols[..., None] * col_freq % box).astype(jnp.float32) * (
        -2.0 * math.pi / box
    )
    row_cos = jnp.cos(row_angle)[..., :, None]
    row_sin = jnp.sin(row_angle)[..., :, None]
    col_cos = jnp.cos(col_angle)[..., None, :]
    col_sin = jnp.sin(col_angle)[..., None, :]
    phase_re = row_cos * col_cos - row_sin * col_sin
    phase_im = row_cos * col_sin + row_sin * col_cos
    return (phase_re, phase_im)


def contrast(defocus_vals, row_freq, col_freq, box):
    radius = (row_freq[:, None] * row_freq[:, None] + col_freq[None, :] * col_freq[None, :]).astype(
        jnp.float32
    ) / float(box * box)
    return -jnp.sin(200.0 * defocus_vals[:, None, None] * radius[None] + 0.1)


def aligned_rows(block_images, gain, block_offsets, row_freq, col_freq, box):
    phase_re, phase_im = wave_tables(
        block_offsets[..., 0], block_offsets[..., 1], row_freq, col_freq, box
    )
    scaled = gain[:, None]
    real_part = block_images[:, 0].astype(jnp.float32)[:, None]
    imag_part = block_images[:, 1].astype(jnp.float32)[:, None]
    aligned_re = scaled * (real_part * phase_re - imag_part * phase_im)
    aligned_im = scaled * (real_part * phase_im + imag_part * phase_re)
    stacked = jnp.stack([aligned_re, aligned_im], axis=3).astype(jnp.bfloat16)
    return stacked.reshape(stacked.shape[0] * stacked.shape[1], -1)


def correlate(aligned, panel):
    return lax.dot_general(
        aligned, panel, (((1,), (1,)), ((), ())), preferred_element_type=jnp.float32
    )


def per_device(images, defocus, references, offsets, posterior, class_ids, seg_count):
    seg_dev = images.shape[0]
    rows = images.shape[2]
    cols = images.shape[3]
    box = FROWS
    row_first = lax.axis_index("row") * rows
    row_freq = (row_first + jnp.arange(rows, dtype=jnp.int32) + box // 2) % box - box // 2
    col_freq = jnp.arange(cols, dtype=jnp.int32)
    live = (
        (jnp.arange(SEG_FIL, dtype=jnp.int32)[None, :] < seg_count[:, None])
        .reshape(-1)
        .astype(jnp.float32)
    )
    weight = live[:, None] * posterior.astype(jnp.float32) / 256.0
    local_panel = jnp.transpose(references, (0, 2, 1, 3)).reshape(references.shape[0], -1)
    classes = jnp.arange(CLASSES, dtype=jnp.int32)
    blocks = seg_dev // 8
    panel = lax.all_gather(local_panel, "fil", axis=0, tiled=True)

    def step(carry, inputs):
        numer, denom = carry
        block_images, block_defocus, block_offsets, block_weight, block_live, block_ids = inputs
        ctf = contrast(block_defocus, row_freq, col_freq, box)
        aligned = aligned_rows(
            block_images, ctf * block_live[:, None, None], block_offsets, row_freq, col_freq, box
        )
        block_scores = correlate(aligned, panel)
        member = (block_ids[None, :] == classes[:, None]).astype(jnp.float32)
        spread = (member[:, :, None] * block_weight[None]).astype(jnp.bfloat16).reshape(CLASSES, -1)
        numer = numer + jnp.dot(spread, aligned, preferred_element_type=jnp.float32)
        totals = member * jnp.sum(block_weight, axis=1)[None, :]
        denom = denom + jnp.dot(
            totals,
            (ctf * ctf).reshape(ctf.shape[0], -1),
            precision=lax.Precision.HIGHEST,
            preferred_element_type=jnp.float32,
        )
        return ((numer, denom), block_scores.reshape(8, SHIFTS, -1))

    inputs = (
        images.reshape(blocks, 8, 2, rows, cols),
        defocus.reshape(blocks, 8),
        offsets.reshape(blocks, 8, SHIFTS, 2),
        weight.reshape(blocks, 8, SHIFTS),
        live.reshape(blocks, 8),
        class_ids.reshape(blocks, 8),
    )
    start = (
        jnp.zeros((CLASSES, rows * 2 * cols), jnp.float32),
        jnp.zeros((CLASSES, rows * cols), jnp.float32),
    )
    (numer, denom), partial_scores = lax.scan(step, start, inputs)
    scores = lax.psum_scatter(
        partial_scores.reshape(seg_dev, SHIFTS, -1), "row", scatter_dimension=1, tiled=True
    )
    share = rows * 2 * cols // lax.axis_size("fil")
    total_numer, total_denom = lax.psum((numer, denom), "fil")
    wide = jnp.broadcast_to(
        total_denom.reshape(CLASSES, rows, 1, cols), (CLASSES, rows, 2, cols)
    ).reshape(CLASSES, -1)
    whole_avg = total_numer * lax.rsqrt(wide + 1.0)
    averages = lax.dynamic_slice_in_dim(whole_avg, lax.axis_index("fil") * share, share, 1)
    return (scores, averages)


SINE = (
    6.283185139080197,
    -41.34161488788259,
    81.60061435566797,
    -76.62117706362086,
    41.37130756865165,
    -12.514333309608835,
)
DEFOCUS, TOTAL, LIVE = 16, 17, 18


def sine_turns(turns):
    r = turns - jnp.round(turns)
    z = r * r
    p = jnp.full_like(z, SINE[-1])
    for c in SINE[-2::-1]:
        p = p * z + c
    return p * r


def floats(shape, axis):
    return lax.broadcasted_iota(jnp.int32, shape, axis).astype(jnp.float32)


def split(x):
    hi = x.astype(jnp.bfloat16)
    return hi, (x - hi.astype(jnp.float32)).astype(jnp.bfloat16)


def mm(a, b, contract_a=1):
    return lax.dot_general(
        a, b, (((contract_a,), (0,)), ((), ())), preferred_element_type=jnp.float32
    )


def ctf_of(defocus, kw, kx, box):
    radius = (kw * kw + kx * kx) * (1.0 / (box * box))
    arg = 200.0 * defocus * radius + 0.1
    return -sine_turns(arg * (0.5 / math.pi))


def fused(
    fils,
    row_devs,
    img,
    refs,
    tile,
    cols,
    scores_out,
    avg_out,
    refs_all,
    tiles_all,
    pf,
    pbuf,
    precv,
    fbuf,
    yscr,
    sbuf,
    srecv,
    ref_send,
    ref_recv,
    tile_send,
    tile_recv,
    p_send,
    p_recv,
    s_send,
    s_recv,
):
    segs, _, rows, kcols = img.shape
    box = FROWS
    own = rows // fils
    fil = lax.axis_index("fil")
    row = lax.axis_index("row")

    def fil_peer(k):
        return lax.rem(fil + k, fils)

    def row_peer(k):
        return lax.rem(row + k, row_devs)

    barrier = pltpu.get_barrier_semaphore()
    for k in range(1, fils):
        pl.semaphore_signal(barrier, inc=1, device_id=(fil_peer(k), row), device_id_type=MESH)
    for k in range(1, row_devs):
        pl.semaphore_signal(barrier, inc=1, device_id=(fil, row_peer(k)), device_id_type=MESH)
    pl.semaphore_wait(barrier, fils + row_devs - 2)

    def to_fil(k, src, dst_all, send, recv):
        return pltpu.make_async_remote_copy(
            src_ref=src,
            dst_ref=dst_all.at[fil],
            send_sem=send.at[k],
            recv_sem=recv.at[fil],
            device_id=(fil_peer(k), row),
            device_id_type=MESH,
        )

    def from_fil(k, dst_all, send, recv):
        d = fil_peer(k)
        return pltpu.make_async_remote_copy(
            src_ref=dst_all.at[d],
            dst_ref=dst_all.at[d],
            send_sem=send.at[k],
            recv_sem=recv.at[d],
            device_id=(d, row),
            device_id_type=MESH,
        )

    tile_copies = [to_fil(k, tile, tiles_all, tile_send, tile_recv) for k in range(1, fils)]
    ref_copies = [to_fil(k, refs, refs_all, ref_send, ref_recv) for k in range(1, fils)]
    for c in tile_copies + ref_copies:
        c.start()
    tiles_all[fil] = tile[...]
    refs_all[fil] = refs[...]

    pairs = segs * SHIFTS
    sy = cols[:, 0:1]
    sx = cols[:, 1:2]
    wt = cols[:, 2:3]
    lane = lax.broadcasted_iota(jnp.int32, (1, 2 * rows), 1)
    ky = (row * rows + lax.rem(lane, rows)).astype(jnp.float32)
    kw = jnp.where(ky >= box // 2, ky - box, ky)
    low = lane < rows
    q = -(sy * kw)
    wave_a = sine_turns((q + jnp.where(low, 64.0, 128.0)) * (1.0 / box))
    wave_b = sine_turns((q + jnp.where(low, 0.0, 64.0)) * (1.0 / box))
    kx = floats((1, kcols), 1)
    qc = -(sx * kx)
    col_cos = sine_turns((qc + 64.0) * (1.0 / box))
    col_sin = sine_turns(qc * (1.0 / box))

    a_hi, a_lo = split(wave_a)
    b_hi, b_lo = split(wave_b)
    c_hi, c_lo = split(jnp.concatenate([col_cos * wt, col_sin * wt], axis=1))

    kyl = (row * rows).astype(jnp.float32) + floats((rows, 1), 0)
    kwl = jnp.where(kyl >= box // 2, kyl - box, kyl)
    gains = []
    for i in range(segs):
        ctf = ctf_of(tile[i : i + 1, DEFOCUS : DEFOCUS + 1], kwl, kx, box)
        g = ctf * tile[i : i + 1, LIVE : LIVE + 1]
        g_re = g * img[i, 0].astype(jnp.float32)
        g_im = g * img[i, 1].astype(jnp.float32)
        gains.append((g_re, g_im))
        at = slice(i * SHIFTS, (i + 1) * SHIFTS)
        grid = mm(
            jnp.concatenate([a_hi[at], a_hi[at], a_lo[at]], axis=0),
            jnp.concatenate([c_hi[at], c_lo[at], c_hi[at]], axis=0),
            contract_a=0,
        )
        w_re = grid[:rows, :kcols] + grid[rows:, kcols:]
        w_im = grid[:rows, kcols:] - grid[rows:, :kcols]
        p_re = g_re * w_re - g_im * w_im
        p_im = g_re * w_im + g_im * w_re
        for d in range(fils):
            part = slice(d * own, (d + 1) * own)
            pf[d, pl.ds(i, own, stride=2 * segs), :] = p_re[part]
            pf[d, pl.ds(segs + i, own, stride=2 * segs), :] = p_im[part]

    p_copies = []
    for k in range(1, fils):
        d = fil_peer(k)
        pbuf[d] = pf[d].astype(jnp.bfloat16)
        c = to_fil(k, pbuf.at[d], precv, p_send, p_recv)
        c.start()
        p_copies.append(c)
    precv[fil] = pf[fil].astype(jnp.bfloat16)

    for k in range(1, fils):
        from_fil(k, refs_all, ref_send, ref_recv).wait_recv()
    for i in range(segs):
        at = slice(i * SHIFTS, (i + 1) * SHIFTS)
        lhs = jnp.concatenate([a_hi[at], b_hi[at], a_lo[at], b_lo[at]], axis=0)
        g_re, g_im = gains[i]
        for r in range(0, fils, 2):
            panel = []
            for e in (r, r + 1):
                f_re = refs_all[e, 0].astype(jnp.float32)
                f_im = refs_all[e, 1].astype(jnp.float32)
                q_re = g_re * f_re + g_im * f_im
                q_im = g_im * f_re - g_re * f_im
                panel.append(jnp.concatenate([q_re, q_im], axis=0).astype(jnp.bfloat16))
            z = mm(lhs, jnp.concatenate(panel, axis=1))
            z = z[: 2 * SHIFTS] + z[2 * SHIFTS :]
            for e in (0, 1):
                ze = z[:, e * kcols : (e + 1) * kcols]
                fbuf[at, (r + e) * kcols : (r + e + 1) * kcols] = (
                    col_cos[at] * ze[:SHIFTS] - col_sin[at] * ze[SHIFTS:]
                )
    f_hi, f_lo = split(fbuf[...])
    wide = (fils * kcols, 128)
    ones = (
        lax.broadcasted_iota(jnp.int32, wide, 0) // kcols
        == lax.rem(lax.broadcasted_iota(jnp.int32, wide, 1), fils)
    ).astype(jnp.bfloat16)
    spread = mm(f_hi, ones) + mm(f_lo, ones)
    per = SHIFTS // row_devs
    pick = (
        lax.broadcasted_iota(jnp.int32, (per, 128), 1) // fils
        == lax.broadcasted_iota(jnp.int32, (per, 128), 0)
    ).astype(jnp.float32)
    yscr[...] = jnp.sum(spread.reshape(pairs // per, per, 128) * pick[None], axis=1)
    for j in range(row_devs):
        sbuf[j] = yscr[pl.ds(j, segs, stride=row_devs), :]
    s_copies = []
    for k in range(1, row_devs):
        c = pltpu.make_async_remote_copy(
            src_ref=sbuf.at[row_peer(k)],
            dst_ref=srecv.at[row],
            send_sem=s_send.at[k],
            recv_sem=s_recv.at[row],
            device_id=(fil, row_peer(k)),
            device_id_type=MESH,
        )
        c.start()
        s_copies.append(c)

    for k in range(1, fils):
        from_fil(k, tiles_all, tile_send, tile_recv).wait_recv()
    every = fils * segs
    tiles = tiles_all[...].reshape(every, 128)
    member = jnp.transpose(tiles)[:CLASSES].astype(jnp.bfloat16)
    defocus = tiles[:, DEFOCUS : DEFOCUS + 1]
    total = tiles[:, TOTAL : TOTAL + 1]
    squares = []
    for y in range(own):
        k0 = (row * rows + fil * own + y).astype(jnp.float32)
        k0 = jnp.where(k0 >= box // 2, k0 - box, k0)
        ctf = ctf_of(defocus, k0, kx, box)
        squares.append(total * (ctf * ctf))
    d_hi, d_lo = split(jnp.concatenate(squares, axis=1))
    denom = mm(member, d_hi) + mm(member, d_lo)
    scale = lax.rsqrt(denom + 1.0)

    for k in range(1, fils):
        from_fil(k, precv, p_send, p_recv).wait_recv()
    parts = precv[...].astype(jnp.float32).reshape(fils, 2 * own, segs, kcols)
    for y in range(own):
        for part in range(2):
            t = 2 * y + part
            rhs = parts[:, t].reshape(every, kcols).astype(jnp.bfloat16)
            avg_out[:, t * kcols : (t + 1) * kcols] = (
                mm(member, rhs) * scale[:, y * kcols : (y + 1) * kcols]
            )

    acc = sbuf[row]
    for k in range(1, row_devs):
        q = row_peer(k)
        pltpu.make_async_remote_copy(
            src_ref=srecv.at[q],
            dst_ref=srecv.at[q],
            send_sem=s_send.at[k],
            recv_sem=s_recv.at[q],
            device_id=(fil, q),
            device_id_type=MESH,
        ).wait_recv()
        acc = acc + srecv[q]
    scores_out[...] = acc
    for c in tile_copies + ref_copies + p_copies + s_copies:
        c.wait_send()


def per_device_fused(images, defocus, references, offsets, posterior, class_ids, seg_count):
    segs, _, rows, kcols = images.shape
    fils = lax.axis_size("fil")
    row_devs = lax.axis_size("row")
    live = (jnp.arange(SEG_FIL, dtype=jnp.int32) < seg_count).astype(jnp.float32)
    weight = posterior.astype(jnp.float32) / 256.0
    member = (class_ids[:, None] == jnp.arange(CLASSES, dtype=jnp.int32)[None]).astype(jnp.float32)
    numbers = jnp.stack([defocus, live * jnp.sum(weight, axis=1), live], axis=1)
    tile = jnp.pad(jnp.concatenate([member, numbers], axis=1), ((0, 0), (0, 125 - CLASSES)))
    shifts = offsets.astype(jnp.float32).reshape(segs * SHIFTS, 2)
    cols = jnp.concatenate([shifts, weight.reshape(segs * SHIFTS, 1)], axis=1)
    own = rows // fils
    block = 2 * own * segs
    per = SHIFTS // row_devs
    vmem = pl.BlockSpec(memory_space=pltpu.VMEM)
    dma = pltpu.SemaphoreType.DMA

    def kernel(*refs):
        fused(fils, row_devs, *refs)

    scores, averages = pl.pallas_call(
        kernel,
        out_shape=(
            jax.ShapeDtypeStruct((segs, 128), jnp.float32),
            jax.ShapeDtypeStruct((CLASSES, 2 * own * kcols), jnp.float32),
        ),
        in_specs=[vmem] * 4,
        out_specs=(vmem, vmem),
        scratch_shapes=[
            pltpu.VMEM((fils, 2, rows, kcols), jnp.bfloat16),
            pltpu.VMEM((fils, segs, 128), jnp.float32),
            pltpu.VMEM((fils, block, kcols), jnp.float32),
            pltpu.VMEM((fils, block, kcols), jnp.bfloat16),
            pltpu.VMEM((fils, block, kcols), jnp.bfloat16),
            pltpu.VMEM((segs * SHIFTS, fils * kcols), jnp.float32),
            pltpu.VMEM((segs * row_devs, 128), jnp.float32),
            pltpu.VMEM((row_devs, segs, 128), jnp.float32),
            pltpu.VMEM((row_devs, segs, 128), jnp.float32),
            dma((fils,)),
            dma((fils,)),
            dma((fils,)),
            dma((fils,)),
            dma((fils,)),
            dma((fils,)),
            dma((row_devs,)),
            dma((row_devs,)),
        ],
        compiler_params=pltpu.CompilerParams(
            collective_id=0, has_side_effects=True, vmem_limit_bytes=32 * 1024 * 1024
        ),
    )(images, references[0], tile, cols)
    return scores[:, : per * fils].reshape(segs, per, fils), averages


def fits(mesh):
    fils, row_devs = mesh.shape["fil"], mesh.shape["row"]
    return fils == 8 and FROWS == 8 * fils * row_devs and SHIFTS == 8 * row_devs


def solution(mesh):
    placed = (
        P("fil", None, "row", None),
        P("fil"),
        P("fil", None, "row", None),
        P("fil", None, None),
        P("fil", None),
        P("fil"),
        P("fil"),
    )
    return jax.shard_map(
        per_device_fused if fits(mesh) else per_device,
        mesh=mesh,
        in_specs=placed,
        out_specs=(P("fil", "row", None), P(None, ("row", "fil"))),
        check_vma=False,
    )
```

```python
import math

import jax
import jax.numpy as jnp
from jax import lax
from jax.experimental import pallas as pl
from jax.experimental.pallas import tpu as pltpu
from jax.sharding import PartitionSpec as P

MESH = pl.DeviceIdType.MESH

FROWS = 256
SHIFTS = 32
CLASSES = 16
SEG_FIL = 8


def wave_tables(shift_rows, shift_cols, row_freq, col_freq, box):
    row_angle = (shift_rows[..., None] * row_freq % box).astype(jnp.float32) * (
        -2.0 * math.pi / box
    )
    col_angle = (shift_cols[..., None] * col_freq % box).astype(jnp.float32) * (
        -2.0 * math.pi / box
    )
    row_cos = jnp.cos(row_angle)[..., :, None]
    row_sin = jnp.sin(row_angle)[..., :, None]
    col_cos = jnp.cos(col_angle)[..., None, :]
    col_sin = jnp.sin(col_angle)[..., None, :]
    phase_re = row_cos * col_cos - row_sin * col_sin
    phase_im = row_cos * col_sin + row_sin * col_cos
    return (phase_re, phase_im)


def contrast(defocus_vals, row_freq, col_freq, box):
    radius = (row_freq[:, None] * row_freq[:, None] + col_freq[None, :] * col_freq[None, :]).astype(
        jnp.float32
    ) / float(box * box)
    return -jnp.sin(200.0 * defocus_vals[:, None, None] * radius[None] + 0.1)


def aligned_rows(block_images, gain, block_offsets, row_freq, col_freq, box):
    phase_re, phase_im = wave_tables(
        block_offsets[..., 0], block_offsets[..., 1], row_freq, col_freq, box
    )
    scaled = gain[:, None]
    real_part = block_images[:, 0].astype(jnp.float32)[:, None]
    imag_part = block_images[:, 1].astype(jnp.float32)[:, None]
    aligned_re = scaled * (real_part * phase_re - imag_part * phase_im)
    aligned_im = scaled * (real_part * phase_im + imag_part * phase_re)
    stacked = jnp.stack([aligned_re, aligned_im], axis=3).astype(jnp.bfloat16)
    return stacked.reshape(stacked.shape[0] * stacked.shape[1], -1)


def correlate(aligned, panel):
    return lax.dot_general(
        aligned, panel, (((1,), (1,)), ((), ())), preferred_element_type=jnp.float32
    )


def per_device(images, defocus, references, offsets, posterior, class_ids, seg_count):
    seg_dev = images.shape[0]
    rows = images.shape[2]
    cols = images.shape[3]
    box = FROWS
    row_first = lax.axis_index("row") * rows
    row_freq = (row_first + jnp.arange(rows, dtype=jnp.int32) + box // 2) % box - box // 2
    col_freq = jnp.arange(cols, dtype=jnp.int32)
    live = (
        (jnp.arange(SEG_FIL, dtype=jnp.int32)[None, :] < seg_count[:, None])
        .reshape(-1)
        .astype(jnp.float32)
    )
    weight = live[:, None] * posterior.astype(jnp.float32) / 256.0
    local_panel = jnp.transpose(references, (0, 2, 1, 3)).reshape(references.shape[0], -1)
    classes = jnp.arange(CLASSES, dtype=jnp.int32)
    blocks = seg_dev // 8
    panel = lax.all_gather(local_panel, "fil", axis=0, tiled=True)

    def step(carry, inputs):
        numer, denom = carry
        block_images, block_defocus, block_offsets, block_weight, block_live, block_ids = inputs
        ctf = contrast(block_defocus, row_freq, col_freq, box)
        aligned = aligned_rows(
            block_images, ctf * block_live[:, None, None], block_offsets, row_freq, col_freq, box
        )
        block_scores = correlate(aligned, panel)
        member = (block_ids[None, :] == classes[:, None]).astype(jnp.float32)
        spread = (member[:, :, None] * block_weight[None]).astype(jnp.bfloat16).reshape(CLASSES, -1)
        numer = numer + jnp.dot(spread, aligned, preferred_element_type=jnp.float32)
        totals = member * jnp.sum(block_weight, axis=1)[None, :]
        denom = denom + jnp.dot(
            totals,
            (ctf * ctf).reshape(ctf.shape[0], -1),
            precision=lax.Precision.HIGHEST,
            preferred_element_type=jnp.float32,
        )
        return ((numer, denom), block_scores.reshape(8, SHIFTS, -1))

    inputs = (
        images.reshape(blocks, 8, 2, rows, cols),
        defocus.reshape(blocks, 8),
        offsets.reshape(blocks, 8, SHIFTS, 2),
        weight.reshape(blocks, 8, SHIFTS),
        live.reshape(blocks, 8),
        class_ids.reshape(blocks, 8),
    )
    start = (
        jnp.zeros((CLASSES, rows * 2 * cols), jnp.float32),
        jnp.zeros((CLASSES, rows * cols), jnp.float32),
    )
    (numer, denom), partial_scores = lax.scan(step, start, inputs)
    scores = lax.psum_scatter(
        partial_scores.reshape(seg_dev, SHIFTS, -1), "row", scatter_dimension=1, tiled=True
    )
    share = rows * 2 * cols // lax.axis_size("fil")
    total_numer, total_denom = lax.psum((numer, denom), "fil")
    wide = jnp.broadcast_to(
        total_denom.reshape(CLASSES, rows, 1, cols), (CLASSES, rows, 2, cols)
    ).reshape(CLASSES, -1)
    whole_avg = total_numer * lax.rsqrt(wide + 1.0)
    averages = lax.dynamic_slice_in_dim(whole_avg, lax.axis_index("fil") * share, share, 1)
    return (scores, averages)


SINE = (
    6.283185139080197,
    -41.34161488788259,
    81.60061435566797,
    -76.62117706362086,
    41.37130756865165,
    -12.514333309608835,
)
DEFOCUS, TOTAL, LIVE = 16, 17, 18


def sine_turns(turns):
    r = turns - jnp.round(turns)
    z = r * r
    p = jnp.full_like(z, SINE[-1])
    for c in SINE[-2::-1]:
        p = p * z + c
    return p * r


def floats(shape, axis):
    return lax.broadcasted_iota(jnp.int32, shape, axis).astype(jnp.float32)


def split(x):
    hi = x.astype(jnp.bfloat16)
    return hi, (x - hi.astype(jnp.float32)).astype(jnp.bfloat16)


def mm(a, b, contract_a=1):
    return lax.dot_general(
        a, b, (((contract_a,), (0,)), ((), ())), preferred_element_type=jnp.float32
    )


def ctf_of(defocus, kw, kx, box):
    radius = (kw * kw + kx * kx) * (1.0 / (box * box))
    arg = 200.0 * defocus * radius + 0.1
    return -sine_turns(arg * (0.5 / math.pi))


def fused(
    fils,
    row_devs,
    img_hbm,
    refs,
    offsets_hbm,
    posterior_hbm,
    defocus_hbm,
    ids_hbm,
    count_hbm,
    scores_out,
    avg_out,
    img,
    offsets,
    posterior,
    defocus_in,
    ids_in,
    count_in,
    turned,
    tile,
    refs_all,
    tiles_all,
    pf,
    pbuf,
    precv,
    fbuf,
    yscr,
    sbuf,
    srecv,
    ref_send,
    ref_recv,
    tile_send,
    tile_recv,
    p_send,
    p_recv,
    s_send,
    s_recv,
    in_sem,
):
    segs, _, rows, kcols = img.shape
    box = FROWS
    own = rows // fils
    fil = lax.axis_index("fil")
    row = lax.axis_index("row")

    def fil_peer(k):
        return lax.rem(fil + k, fils)

    def row_peer(k):
        return lax.rem(row + k, row_devs)

    barrier = pltpu.get_barrier_semaphore()
    for k in range(1, fils):
        pl.semaphore_signal(barrier, inc=1, device_id=(fil_peer(k), row), device_id_type=MESH)
    for k in range(1, row_devs):
        pl.semaphore_signal(barrier, inc=1, device_id=(fil, row_peer(k)), device_id_type=MESH)
    pulls = [
        pltpu.make_async_copy(src, dst, in_sem.at[j])
        for j, (src, dst) in enumerate(
            (
                (offsets_hbm, offsets),
                (posterior_hbm, posterior),
                (defocus_hbm, defocus_in),
                (ids_hbm, ids_in),
                (count_hbm, count_in),
                (img_hbm, img),
                (refs, refs_all.at[fil]),
            )
        )
    ]
    for c in pulls:
        c.start()
    pl.semaphore_wait(barrier, fils + row_devs - 2)

    def to_fil(k, src, dst_all, send, recv):
        return pltpu.make_async_remote_copy(
            src_ref=src,
            dst_ref=dst_all.at[fil],
            send_sem=send.at[k],
            recv_sem=recv.at[fil],
            device_id=(fil_peer(k), row),
            device_id_type=MESH,
        )

    def from_fil(k, dst_all, send, recv):
        d = fil_peer(k)
        return pltpu.make_async_remote_copy(
            src_ref=dst_all.at[d],
            dst_ref=dst_all.at[d],
            send_sem=send.at[k],
            recv_sem=recv.at[d],
            device_id=(d, row),
            device_id_type=MESH,
        )

    partner = fil + 1 - 2 * lax.rem(fil, 2)
    ref_copies = []
    for k in range(fils // 2, 0, -1):
        d = fil_peer(2 * k) if 2 * k < fils else partner
        ref_copies.append(
            pltpu.make_async_remote_copy(
                src_ref=refs,
                dst_ref=refs_all.at[fil],
                send_sem=ref_send.at[k],
                recv_sem=ref_recv.at[fil],
                device_id=(d, row),
                device_id_type=MESH,
            )
        )
    for c in ref_copies:
        c.start()

    for c in pulls[:5]:
        c.wait()
    turned[...] = jnp.zeros_like(turned)
    shifts = offsets[...].astype(jnp.float32)
    turned[0:segs, 0:SHIFTS] = shifts[:, 0, :]
    turned[segs : 2 * segs, 0:SHIFTS] = shifts[:, 1, :]
    turned[2 * segs : 3 * segs, 0:SHIFTS] = posterior[...].astype(jnp.float32) * (1.0 / 256.0)
    turned[3 * segs : 3 * segs + 1, 0:segs] = ids_in[...].astype(jnp.float32)
    turned[3 * segs + 1 : 3 * segs + 2, 0:segs] = defocus_in[...]
    up = jnp.transpose(turned[...])
    weights = turned[2 * segs : 3 * segs, :]
    live = (floats((segs, 1), 0) < count_in[...].astype(jnp.float32)).astype(jnp.float32)
    sums = live * jnp.sum(weights, axis=1, keepdims=True)
    ids_col = up[0:segs, 3 * segs : 3 * segs + 1]
    def_col = up[0:segs, 3 * segs + 1 : 3 * segs + 2]
    at_lane = floats((segs, 128), 1)
    hot = jnp.where(ids_col == at_lane, 1.0, 0.0)
    tile[...] = jnp.where(
        at_lane == DEFOCUS,
        def_col,
        jnp.where(at_lane == TOTAL, sums, jnp.where(at_lane == LIVE, live, hot)),
    )
    tile_copies = [to_fil(k, tile, tiles_all, tile_send, tile_recv) for k in range(1, fils)]
    for c in tile_copies:
        c.start()
    tiles_all[fil] = tile[...]

    pairs = segs * SHIFTS

    def column(j):
        first = j * segs
        return jnp.concatenate(
            [up[0:SHIFTS, first + i : first + i + 1] for i in range(segs)], axis=0
        )

    sy, sx, wt = column(0), column(1), column(2)
    lane = lax.broadcasted_iota(jnp.int32, (1, 2 * rows), 1)
    ky = (row * rows + lax.rem(lane, rows)).astype(jnp.float32)
    kw = jnp.where(ky >= box // 2, ky - box, ky)
    low = lane < rows
    q = -(sy * kw)
    wave_a = sine_turns((q + jnp.where(low, 64.0, 128.0)) * (1.0 / box))
    wave_b = sine_turns((q + jnp.where(low, 0.0, 64.0)) * (1.0 / box))
    kx = floats((1, kcols), 1)
    qc = -(sx * kx)
    col_cos = sine_turns((qc + 64.0) * (1.0 / box))
    col_sin = sine_turns(qc * (1.0 / box))

    a_hi, a_lo = split(wave_a)
    b_hi, b_lo = split(wave_b)
    c_hi, c_lo = split(jnp.concatenate([col_cos * wt, col_sin * wt], axis=1))

    kyl = (row * rows).astype(jnp.float32) + floats((rows, 1), 0)
    kwl = jnp.where(kyl >= box // 2, kyl - box, kyl)
    gains = []
    pulls[5].wait()
    for i in range(segs):
        ctf = ctf_of(tile[i : i + 1, DEFOCUS : DEFOCUS + 1], kwl, kx, box)
        g = ctf * tile[i : i + 1, LIVE : LIVE + 1]
        g_re = g * img[i, 0].astype(jnp.float32)
        g_im = g * img[i, 1].astype(jnp.float32)
        gains.append((g_re, g_im))
        at = slice(i * SHIFTS, (i + 1) * SHIFTS)
        grid = mm(
            jnp.concatenate([a_hi[at], a_hi[at], a_lo[at]], axis=0),
            jnp.concatenate([c_hi[at], c_lo[at], c_hi[at]], axis=0),
            contract_a=0,
        )
        w_re = grid[:rows, :kcols] + grid[rows:, kcols:]
        w_im = grid[:rows, kcols:] - grid[rows:, :kcols]
        p_re = g_re * w_re - g_im * w_im
        p_im = g_re * w_im + g_im * w_re
        for d in range(fils):
            part = slice(d * own, (d + 1) * own)
            pf[d, pl.ds(i, own, stride=2 * segs), :] = p_re[part]
            pf[d, pl.ds(segs + i, own, stride=2 * segs), :] = p_im[part]

    p_copies = []
    for k in sorted(range(1, fils), key=lambda k: abs(k - fils // 2)):
        d = fil_peer(k)
        pbuf[d] = pf[d].astype(jnp.bfloat16)
        c = to_fil(k, pbuf.at[d], precv, p_send, p_recv)
        c.start()
        p_copies.append(c)
    precv[fil] = pf[fil].astype(jnp.bfloat16)

    for k in range(2, fils, 2):
        from_fil(k, refs_all, ref_send, ref_recv).wait_recv()
        d = fil_peer(k)
        c = pltpu.make_async_remote_copy(
            src_ref=refs_all.at[d],
            dst_ref=refs_all.at[d],
            send_sem=ref_send.at[fils // 2 + k // 2],
            recv_sem=ref_recv.at[d],
            device_id=(partner, row),
            device_id_type=MESH,
        )
        c.start()
        ref_copies.append(c)

    for k in range(1, fils):
        from_fil(k, tiles_all, tile_send, tile_recv).wait_recv()
    every = fils * segs
    tiles = tiles_all[...].reshape(every, 128)
    member = jnp.transpose(tiles)[:CLASSES].astype(jnp.bfloat16)
    defocus = tiles[:, DEFOCUS : DEFOCUS + 1]
    total = tiles[:, TOTAL : TOTAL + 1]
    squares = []
    for y in range(own):
        k0 = (row * rows + fil * own + y).astype(jnp.float32)
        k0 = jnp.where(k0 >= box // 2, k0 - box, k0)
        ctf = ctf_of(defocus, k0, kx, box)
        squares.append(total * (ctf * ctf))
    d_hi, d_lo = split(jnp.concatenate(squares, axis=1))
    denom = mm(member, d_hi) + mm(member, d_lo)
    scale = lax.rsqrt(denom + 1.0)

    pulls[6].wait()
    for k in range(0, fils // 2):
        d = lax.rem(partner + 2 * k, fils)
        pltpu.make_async_remote_copy(
            src_ref=refs_all.at[d],
            dst_ref=refs_all.at[d],
            send_sem=ref_send.at[0],
            recv_sem=ref_recv.at[d],
            device_id=(partner, row),
            device_id_type=MESH,
        ).wait_recv()
    for i in range(segs):
        at = slice(i * SHIFTS, (i + 1) * SHIFTS)
        lhs = jnp.concatenate([a_hi[at], b_hi[at], a_lo[at], b_lo[at]], axis=0)
        g_re, g_im = gains[i]
        for r in range(0, fils, 2):
            panel = []
            for e in (r, r + 1):
                f_re = refs_all[e, 0].astype(jnp.float32)
                f_im = refs_all[e, 1].astype(jnp.float32)
                q_re = g_re * f_re + g_im * f_im
                q_im = g_im * f_re - g_re * f_im
                panel.append(jnp.concatenate([q_re, q_im], axis=0).astype(jnp.bfloat16))
            z = mm(lhs, jnp.concatenate(panel, axis=1))
            z = z[: 2 * SHIFTS] + z[2 * SHIFTS :]
            for e in (0, 1):
                ze = z[:, e * kcols : (e + 1) * kcols]
                fbuf[at, (r + e) * kcols : (r + e + 1) * kcols] = (
                    col_cos[at] * ze[:SHIFTS] - col_sin[at] * ze[SHIFTS:]
                )
    f_hi, f_lo = split(fbuf[...])
    wide = (fils * kcols, 128)
    ones = (
        lax.broadcasted_iota(jnp.int32, wide, 0) // kcols
        == lax.rem(lax.broadcasted_iota(jnp.int32, wide, 1), fils)
    ).astype(jnp.bfloat16)
    spread = mm(f_hi, ones) + mm(f_lo, ones)
    per = SHIFTS // row_devs
    pick = (
        lax.broadcasted_iota(jnp.int32, (per, 128), 1) // fils
        == lax.broadcasted_iota(jnp.int32, (per, 128), 0)
    ).astype(jnp.float32)
    yscr[...] = jnp.sum(spread.reshape(pairs // per, per, 128) * pick[None], axis=1)
    for j in range(row_devs):
        sbuf[j] = yscr[pl.ds(j, segs, stride=row_devs), :]
    s_copies = []
    for k in range(1, row_devs):
        c = pltpu.make_async_remote_copy(
            src_ref=sbuf.at[row_peer(k)],
            dst_ref=srecv.at[row],
            send_sem=s_send.at[k],
            recv_sem=s_recv.at[row],
            device_id=(fil, row_peer(k)),
            device_id_type=MESH,
        )
        c.start()
        s_copies.append(c)

    for k in range(1, fils):
        from_fil(k, precv, p_send, p_recv).wait_recv()
    parts = precv[...].astype(jnp.float32).reshape(fils, 2 * own, segs, kcols)
    for y in range(own):
        for part in range(2):
            t = 2 * y + part
            rhs = parts[:, t].reshape(every, kcols).astype(jnp.bfloat16)
            avg_out[:, t * kcols : (t + 1) * kcols] = (
                mm(member, rhs) * scale[:, y * kcols : (y + 1) * kcols]
            )

    acc = sbuf[row]
    for k in range(1, row_devs):
        q = row_peer(k)
        pltpu.make_async_remote_copy(
            src_ref=srecv.at[q],
            dst_ref=srecv.at[q],
            send_sem=s_send.at[k],
            recv_sem=s_recv.at[q],
            device_id=(fil, q),
            device_id_type=MESH,
        ).wait_recv()
        acc = acc + srecv[q]
    scores_out[...] = acc
    for c in tile_copies + ref_copies + p_copies + s_copies:
        c.wait_send()


def per_device_fused(images, defocus, references, offsets, posterior, class_ids, seg_count):
    segs, _, rows, kcols = images.shape
    fils = lax.axis_size("fil")
    row_devs = lax.axis_size("row")
    own = rows // fils
    block = 2 * own * segs
    per = SHIFTS // row_devs
    vmem = pl.BlockSpec(memory_space=pltpu.VMEM)
    hbm = pl.BlockSpec(memory_space=pl.ANY)
    dma = pltpu.SemaphoreType.DMA

    def kernel(*refs):
        fused(fils, row_devs, *refs)

    scores, averages = pl.pallas_call(
        kernel,
        out_shape=(
            jax.ShapeDtypeStruct((segs, 128), jnp.float32),
            jax.ShapeDtypeStruct((CLASSES, 2 * own * kcols), jnp.float32),
        ),
        in_specs=[hbm] * 7,
        out_specs=(vmem, vmem),
        scratch_shapes=[
            pltpu.VMEM(images.shape, images.dtype),
            pltpu.VMEM((segs, 2, SHIFTS), jnp.int32),
            pltpu.VMEM((segs, SHIFTS), jnp.int32),
            pltpu.VMEM((1, segs), jnp.float32),
            pltpu.VMEM((1, segs), jnp.int32),
            pltpu.VMEM((1, 1), jnp.int32),
            pltpu.VMEM((128, 128), jnp.float32),
            pltpu.VMEM((segs, 128), jnp.float32),
            pltpu.VMEM((fils, 2, rows, kcols), jnp.bfloat16),
            pltpu.VMEM((fils, segs, 128), jnp.float32),
            pltpu.VMEM((fils, block, kcols), jnp.float32),
            pltpu.VMEM((fils, block, kcols), jnp.bfloat16),
            pltpu.VMEM((fils, block, kcols), jnp.bfloat16),
            pltpu.VMEM((segs * SHIFTS, fils * kcols), jnp.float32),
            pltpu.VMEM((segs * row_devs, 128), jnp.float32),
            pltpu.VMEM((row_devs, segs, 128), jnp.float32),
            pltpu.VMEM((row_devs, segs, 128), jnp.float32),
            dma((fils,)),
            dma((fils,)),
            dma((fils,)),
            dma((fils,)),
            dma((fils,)),
            dma((fils,)),
            dma((row_devs,)),
            dma((row_devs,)),
            dma((7,)),
        ],
        compiler_params=pltpu.CompilerParams(
            collective_id=0, has_side_effects=True, vmem_limit_bytes=60 * 1024 * 1024
        ),
    )(
        images,
        references[0],
        jnp.transpose(offsets, (0, 2, 1)),
        posterior,
        defocus[None],
        class_ids[None],
        seg_count[None],
    )
    return scores[:, : per * fils].reshape(segs, per, fils), averages


def fits(mesh):
    fils, row_devs = mesh.shape["fil"], mesh.shape["row"]
    return fils == 8 and FROWS == 8 * fils * row_devs and SHIFTS == 8 * row_devs


def solution(mesh):
    placed = (
        P("fil", None, "row", None),
        P("fil"),
        P("fil", None, "row", None),
        P("fil", None, None),
        P("fil", None),
        P("fil"),
        P("fil"),
    )
    return jax.shard_map(
        per_device_fused if fits(mesh) else per_device,
        mesh=mesh,
        in_specs=placed,
        out_specs=(P("fil", "row", None), P(None, ("row", "fil"))),
        check_vma=False,
    )
```

```python
import math

import jax
import jax.numpy as jnp
from jax import lax
from jax.experimental import pallas as pl
from jax.experimental.pallas import tpu as pltpu
from jax.sharding import PartitionSpec as P

MESH = pl.DeviceIdType.MESH

FROWS = 256
SHIFTS = 32
CLASSES = 16
SEG_FIL = 8


def wave_tables(shift_rows, shift_cols, row_freq, col_freq, box):
    row_angle = (shift_rows[..., None] * row_freq % box).astype(jnp.float32) * (
        -2.0 * math.pi / box
    )
    col_angle = (shift_cols[..., None] * col_freq % box).astype(jnp.float32) * (
        -2.0 * math.pi / box
    )
    row_cos = jnp.cos(row_angle)[..., :, None]
    row_sin = jnp.sin(row_angle)[..., :, None]
    col_cos = jnp.cos(col_angle)[..., None, :]
    col_sin = jnp.sin(col_angle)[..., None, :]
    phase_re = row_cos * col_cos - row_sin * col_sin
    phase_im = row_cos * col_sin + row_sin * col_cos
    return (phase_re, phase_im)


def contrast(defocus_vals, row_freq, col_freq, box):
    radius = (row_freq[:, None] * row_freq[:, None] + col_freq[None, :] * col_freq[None, :]).astype(
        jnp.float32
    ) / float(box * box)
    return -jnp.sin(200.0 * defocus_vals[:, None, None] * radius[None] + 0.1)


def aligned_rows(block_images, gain, block_offsets, row_freq, col_freq, box):
    phase_re, phase_im = wave_tables(
        block_offsets[..., 0], block_offsets[..., 1], row_freq, col_freq, box
    )
    scaled = gain[:, None]
    real_part = block_images[:, 0].astype(jnp.float32)[:, None]
    imag_part = block_images[:, 1].astype(jnp.float32)[:, None]
    aligned_re = scaled * (real_part * phase_re - imag_part * phase_im)
    aligned_im = scaled * (real_part * phase_im + imag_part * phase_re)
    stacked = jnp.stack([aligned_re, aligned_im], axis=3).astype(jnp.bfloat16)
    return stacked.reshape(stacked.shape[0] * stacked.shape[1], -1)


def correlate(aligned, panel):
    return lax.dot_general(
        aligned, panel, (((1,), (1,)), ((), ())), preferred_element_type=jnp.float32
    )


def per_device(images, defocus, references, offsets, posterior, class_ids, seg_count):
    seg_dev = images.shape[0]
    rows = images.shape[2]
    cols = images.shape[3]
    box = FROWS
    row_first = lax.axis_index("row") * rows
    row_freq = (row_first + jnp.arange(rows, dtype=jnp.int32) + box // 2) % box - box // 2
    col_freq = jnp.arange(cols, dtype=jnp.int32)
    live = (
        (jnp.arange(SEG_FIL, dtype=jnp.int32)[None, :] < seg_count[:, None])
        .reshape(-1)
        .astype(jnp.float32)
    )
    weight = live[:, None] * posterior.astype(jnp.float32) / 256.0
    local_panel = jnp.transpose(references, (0, 2, 1, 3)).reshape(references.shape[0], -1)
    classes = jnp.arange(CLASSES, dtype=jnp.int32)
    blocks = seg_dev // 8
    panel = lax.all_gather(local_panel, "fil", axis=0, tiled=True)

    def step(carry, inputs):
        numer, denom = carry
        block_images, block_defocus, block_offsets, block_weight, block_live, block_ids = inputs
        ctf = contrast(block_defocus, row_freq, col_freq, box)
        aligned = aligned_rows(
            block_images, ctf * block_live[:, None, None], block_offsets, row_freq, col_freq, box
        )
        block_scores = correlate(aligned, panel)
        member = (block_ids[None, :] == classes[:, None]).astype(jnp.float32)
        spread = (member[:, :, None] * block_weight[None]).astype(jnp.bfloat16).reshape(CLASSES, -1)
        numer = numer + jnp.dot(spread, aligned, preferred_element_type=jnp.float32)
        totals = member * jnp.sum(block_weight, axis=1)[None, :]
        denom = denom + jnp.dot(
            totals,
            (ctf * ctf).reshape(ctf.shape[0], -1),
            precision=lax.Precision.HIGHEST,
            preferred_element_type=jnp.float32,
        )
        return ((numer, denom), block_scores.reshape(8, SHIFTS, -1))

    inputs = (
        images.reshape(blocks, 8, 2, rows, cols),
        defocus.reshape(blocks, 8),
        offsets.reshape(blocks, 8, SHIFTS, 2),
        weight.reshape(blocks, 8, SHIFTS),
        live.reshape(blocks, 8),
        class_ids.reshape(blocks, 8),
    )
    start = (
        jnp.zeros((CLASSES, rows * 2 * cols), jnp.float32),
        jnp.zeros((CLASSES, rows * cols), jnp.float32),
    )
    (numer, denom), partial_scores = lax.scan(step, start, inputs)
    scores = lax.psum_scatter(
        partial_scores.reshape(seg_dev, SHIFTS, -1), "row", scatter_dimension=1, tiled=True
    )
    share = rows * 2 * cols // lax.axis_size("fil")
    total_numer, total_denom = lax.psum((numer, denom), "fil")
    wide = jnp.broadcast_to(
        total_denom.reshape(CLASSES, rows, 1, cols), (CLASSES, rows, 2, cols)
    ).reshape(CLASSES, -1)
    whole_avg = total_numer * lax.rsqrt(wide + 1.0)
    averages = lax.dynamic_slice_in_dim(whole_avg, lax.axis_index("fil") * share, share, 1)
    return (scores, averages)


SINE = (
    6.283185139080197,
    -41.34161488788259,
    81.60061435566797,
    -76.62117706362086,
    41.37130756865165,
    -12.514333309608835,
)
NEAREST = 12582912.0
DEFOCUS, TOTAL, LIVE = 16, 17, 18


def sine_turns(turns):
    r = turns - ((turns + NEAREST) - NEAREST)
    z = r * r
    p = jnp.full_like(z, SINE[-1])
    for c in SINE[-2::-1]:
        p = p * z + c
    return p * r


def floats(shape, axis):
    return lax.broadcasted_iota(jnp.int32, shape, axis).astype(jnp.float32)


def split(x):
    hi = x.astype(jnp.bfloat16)
    return hi, (x - hi.astype(jnp.float32)).astype(jnp.bfloat16)


def mm(a, b, contract_a=1):
    return lax.dot_general(
        a, b, (((contract_a,), (0,)), ((), ())), preferred_element_type=jnp.float32
    )


def ctf_of(defocus, kw, kx, box):
    radius = (kw * kw + kx * kx) * (1.0 / (box * box))
    arg = 200.0 * defocus * radius + 0.1
    return -sine_turns(arg * (0.5 / math.pi))


def fused(
    fils,
    row_devs,
    img_hbm,
    refs,
    offsets_hbm,
    posterior_hbm,
    defocus_hbm,
    ids_hbm,
    count_hbm,
    scores_out,
    avg_out,
    img,
    offsets,
    posterior,
    defocus_in,
    ids_in,
    count_in,
    turned,
    tile,
    refs_all,
    tiles_all,
    pf,
    pbuf,
    precv,
    fbuf,
    yscr,
    sbuf,
    srecv,
    ref_send,
    ref_recv,
    tile_send,
    tile_recv,
    p_send,
    p_recv,
    s_send,
    s_recv,
    in_sem,
):
    segs, _, rows, kcols = img.shape
    box = FROWS
    own = rows // fils
    fil = lax.axis_index("fil")
    row = lax.axis_index("row")

    def fil_peer(k):
        return lax.rem(fil + k, fils)

    def row_peer(k):
        return lax.rem(row + k, row_devs)

    barrier = pltpu.get_barrier_semaphore()
    for k in range(1, fils):
        pl.semaphore_signal(barrier, inc=1, device_id=(fil_peer(k), row), device_id_type=MESH)
    for k in range(1, row_devs):
        pl.semaphore_signal(barrier, inc=1, device_id=(fil, row_peer(k)), device_id_type=MESH)
    pulls = [
        pltpu.make_async_copy(src, dst, in_sem.at[j])
        for j, (src, dst) in enumerate(
            (
                (offsets_hbm, offsets),
                (posterior_hbm, posterior),
                (defocus_hbm, defocus_in),
                (ids_hbm, ids_in),
                (count_hbm, count_in),
                (img_hbm, img),
                (refs, refs_all.at[fil]),
            )
        )
    ]
    for c in pulls:
        c.start()

    def to_fil(k, src, dst_all, send, recv):
        return pltpu.make_async_remote_copy(
            src_ref=src,
            dst_ref=dst_all.at[fil],
            send_sem=send.at[k],
            recv_sem=recv.at[fil],
            device_id=(fil_peer(k), row),
            device_id_type=MESH,
        )

    def from_fil(k, dst_all, send, recv):
        d = fil_peer(k)
        return pltpu.make_async_remote_copy(
            src_ref=dst_all.at[d],
            dst_ref=dst_all.at[d],
            send_sem=send.at[k],
            recv_sem=recv.at[d],
            device_id=(d, row),
            device_id_type=MESH,
        )

    for c in pulls[:5]:
        c.wait()
    turned[...] = jnp.zeros_like(turned)
    shifts = offsets[...].astype(jnp.float32)
    turned[0:segs, 0:SHIFTS] = shifts[:, 0, :]
    turned[segs : 2 * segs, 0:SHIFTS] = shifts[:, 1, :]
    turned[2 * segs : 3 * segs, 0:SHIFTS] = posterior[...].astype(jnp.float32) * (1.0 / 256.0)
    turned[3 * segs : 3 * segs + 1, 0:segs] = ids_in[...].astype(jnp.float32)
    turned[3 * segs + 1 : 3 * segs + 2, 0:segs] = defocus_in[...]
    up = jnp.transpose(turned[...])
    weights = turned[2 * segs : 3 * segs, :]
    live = (floats((segs, 1), 0) < count_in[...].astype(jnp.float32)).astype(jnp.float32)
    sums = live * jnp.sum(weights, axis=1, keepdims=True)
    ids_col = up[0:segs, 3 * segs : 3 * segs + 1]
    def_col = up[0:segs, 3 * segs + 1 : 3 * segs + 2]
    at_lane = floats((segs, 128), 1)
    hot = jnp.where(ids_col == at_lane, 1.0, 0.0)
    tile[...] = jnp.where(
        at_lane == DEFOCUS,
        def_col,
        jnp.where(at_lane == TOTAL, sums, jnp.where(at_lane == LIVE, live, hot)),
    )
    tiles_all[fil] = tile[...]

    pairs = segs * SHIFTS

    def column(j):
        first = j * segs
        return jnp.concatenate(
            [up[0:SHIFTS, first + i : first + i + 1] for i in range(segs)], axis=0
        )

    sy, sx, wt = column(0), column(1), column(2)
    lane = lax.broadcasted_iota(jnp.int32, (1, 2 * rows), 1)
    ky = (row * rows + lax.rem(lane, rows)).astype(jnp.float32)
    kw = jnp.where(ky >= box // 2, ky - box, ky)
    low = lane < rows
    q = -(sy * kw)
    wave_a = sine_turns((q + jnp.where(low, 64.0, 128.0)) * (1.0 / box))
    wave_b = sine_turns((q + jnp.where(low, 0.0, 64.0)) * (1.0 / box))
    kx = floats((1, kcols), 1)
    qc = -(sx * kx)
    col_cos = sine_turns((qc + 64.0) * (1.0 / box))
    col_sin = sine_turns(qc * (1.0 / box))

    pl.semaphore_wait(barrier, fils + row_devs - 2)
    partner = fil + 1 - 2 * lax.rem(fil, 2)
    ref_copies = []
    for k in range(fils // 2, 0, -1):
        d = fil_peer(2 * k) if 2 * k < fils else partner
        ref_copies.append(
            pltpu.make_async_remote_copy(
                src_ref=refs,
                dst_ref=refs_all.at[fil],
                send_sem=ref_send.at[k],
                recv_sem=ref_recv.at[fil],
                device_id=(d, row),
                device_id_type=MESH,
            )
        )
    for c in ref_copies:
        c.start()
    tile_copies = [to_fil(k, tile, tiles_all, tile_send, tile_recv) for k in range(1, fils)]
    for c in tile_copies:
        c.start()

    a_hi, a_lo = split(wave_a)
    b_hi, b_lo = split(wave_b)
    c_hi, c_lo = split(jnp.concatenate([col_cos * wt, col_sin * wt], axis=1))

    kyl = (row * rows).astype(jnp.float32) + floats((rows, 1), 0)
    kwl = jnp.where(kyl >= box // 2, kyl - box, kyl)
    gains = []
    pulls[5].wait()
    for i in range(segs):
        ctf = ctf_of(tile[i : i + 1, DEFOCUS : DEFOCUS + 1], kwl, kx, box)
        g = ctf * tile[i : i + 1, LIVE : LIVE + 1]
        g_re = g * img[i, 0].astype(jnp.float32)
        g_im = g * img[i, 1].astype(jnp.float32)
        gains.append((g_re, g_im))
        at = slice(i * SHIFTS, (i + 1) * SHIFTS)
        grid = mm(
            jnp.concatenate([a_hi[at], a_hi[at], a_lo[at]], axis=0),
            jnp.concatenate([c_hi[at], c_lo[at], c_hi[at]], axis=0),
            contract_a=0,
        )
        w_re = grid[:rows, :kcols] + grid[rows:, kcols:]
        w_im = grid[:rows, kcols:] - grid[rows:, :kcols]
        p_re = g_re * w_re - g_im * w_im
        p_im = g_re * w_im + g_im * w_re
        for d in range(fils):
            part = slice(d * own, (d + 1) * own)
            pf[d, pl.ds(i, own, stride=2 * segs), :] = p_re[part]
            pf[d, pl.ds(segs + i, own, stride=2 * segs), :] = p_im[part]

    p_copies = []
    for k in sorted(range(1, fils), key=lambda k: abs(k - fils // 2)):
        d = fil_peer(k)
        pbuf[d] = pf[d].astype(jnp.bfloat16)
        c = to_fil(k, pbuf.at[d], precv, p_send, p_recv)
        c.start()
        p_copies.append(c)
    precv[fil] = pf[fil].astype(jnp.bfloat16)

    for k in range(2, fils, 2):
        from_fil(k, refs_all, ref_send, ref_recv).wait_recv()
        d = fil_peer(k)
        c = pltpu.make_async_remote_copy(
            src_ref=refs_all.at[d],
            dst_ref=refs_all.at[d],
            send_sem=ref_send.at[fils // 2 + k // 2],
            recv_sem=ref_recv.at[d],
            device_id=(partner, row),
            device_id_type=MESH,
        )
        c.start()
        ref_copies.append(c)

    for k in range(1, fils):
        from_fil(k, tiles_all, tile_send, tile_recv).wait_recv()
    every = fils * segs
    tiles = tiles_all[...].reshape(every, 128)
    member = jnp.transpose(tiles)[:CLASSES].astype(jnp.bfloat16)
    defocus = tiles[:, DEFOCUS : DEFOCUS + 1]
    total = tiles[:, TOTAL : TOTAL + 1]
    squares = []
    for y in range(own):
        k0 = (row * rows + fil * own + y).astype(jnp.float32)
        k0 = jnp.where(k0 >= box // 2, k0 - box, k0)
        ctf = ctf_of(defocus, k0, kx, box)
        squares.append(total * (ctf * ctf))
    d_hi, d_lo = split(jnp.concatenate(squares, axis=1))
    denom = mm(member, d_hi) + mm(member, d_lo)
    scale = lax.rsqrt(denom + 1.0)

    pulls[6].wait()
    for k in range(0, fils // 2):
        d = lax.rem(partner + 2 * k, fils)
        pltpu.make_async_remote_copy(
            src_ref=refs_all.at[d],
            dst_ref=refs_all.at[d],
            send_sem=ref_send.at[0],
            recv_sem=ref_recv.at[d],
            device_id=(partner, row),
            device_id_type=MESH,
        ).wait_recv()
    for i in range(segs):
        at = slice(i * SHIFTS, (i + 1) * SHIFTS)
        lhs = jnp.concatenate([a_hi[at], b_hi[at], a_lo[at], b_lo[at]], axis=0)
        g_re, g_im = gains[i]
        for r in range(0, fils, 2):
            panel = []
            for e in (r, r + 1):
                f_re = refs_all[e, 0].astype(jnp.float32)
                f_im = refs_all[e, 1].astype(jnp.float32)
                q_re = g_re * f_re + g_im * f_im
                q_im = g_im * f_re - g_re * f_im
                panel.append(jnp.concatenate([q_re, q_im], axis=0).astype(jnp.bfloat16))
            z = mm(lhs, jnp.concatenate(panel, axis=1))
            z = z[: 2 * SHIFTS] + z[2 * SHIFTS :]
            for e in (0, 1):
                ze = z[:, e * kcols : (e + 1) * kcols]
                fbuf[at, (r + e) * kcols : (r + e + 1) * kcols] = (
                    col_cos[at] * ze[:SHIFTS] - col_sin[at] * ze[SHIFTS:]
                )
    f_hi, f_lo = split(fbuf[...])
    lane = lax.broadcasted_iota(jnp.int32, (1, 128), 1)
    ones = jnp.concatenate(
        [
            jnp.broadcast_to((lane & (fils - 1) == r).astype(jnp.float32), (kcols, 128))
            for r in range(fils)
        ],
        axis=0,
    ).astype(jnp.bfloat16)
    spread = mm(f_hi, ones) + mm(f_lo, ones)
    per = SHIFTS // row_devs
    pick = (
        lax.broadcasted_iota(jnp.int32, (per, 128), 1) // fils
        == lax.broadcasted_iota(jnp.int32, (per, 128), 0)
    ).astype(jnp.float32)
    yscr[...] = jnp.sum(spread.reshape(pairs // per, per, 128) * pick[None], axis=1)
    for j in range(row_devs):
        sbuf[j] = yscr[pl.ds(j, segs, stride=row_devs), :]
    s_copies = []
    for k in range(1, row_devs):
        c = pltpu.make_async_remote_copy(
            src_ref=sbuf.at[row_peer(k)],
            dst_ref=srecv.at[row],
            send_sem=s_send.at[k],
            recv_sem=s_recv.at[row],
            device_id=(fil, row_peer(k)),
            device_id_type=MESH,
        )
        c.start()
        s_copies.append(c)

    for k in range(1, fils):
        from_fil(k, precv, p_send, p_recv).wait_recv()
    parts = precv[...].astype(jnp.float32).reshape(fils, 2 * own, segs, kcols)
    for y in range(own):
        for part in range(2):
            t = 2 * y + part
            rhs = parts[:, t].reshape(every, kcols).astype(jnp.bfloat16)
            avg_out[:, t * kcols : (t + 1) * kcols] = (
                mm(member, rhs) * scale[:, y * kcols : (y + 1) * kcols]
            )

    acc = sbuf[row]
    for k in range(1, row_devs):
        q = row_peer(k)
        pltpu.make_async_remote_copy(
            src_ref=srecv.at[q],
            dst_ref=srecv.at[q],
            send_sem=s_send.at[k],
            recv_sem=s_recv.at[q],
            device_id=(fil, q),
            device_id_type=MESH,
        ).wait_recv()
        acc = acc + srecv[q]
    scores_out[...] = acc
    for c in tile_copies + ref_copies + p_copies + s_copies:
        c.wait_send()


def per_device_fused(images, defocus, references, offsets, posterior, class_ids, seg_count):
    segs, _, rows, kcols = images.shape
    fils = lax.axis_size("fil")
    row_devs = lax.axis_size("row")
    own = rows // fils
    block = 2 * own * segs
    per = SHIFTS // row_devs
    vmem = pl.BlockSpec(memory_space=pltpu.VMEM)
    hbm = pl.BlockSpec(memory_space=pltpu.HBM)
    dma = pltpu.SemaphoreType.DMA

    def kernel(*refs):
        fused(fils, row_devs, *refs)

    scores, averages = pl.pallas_call(
        kernel,
        out_shape=(
            jax.ShapeDtypeStruct((segs, 128), jnp.float32),
            jax.ShapeDtypeStruct((CLASSES, 2 * own * kcols), jnp.float32),
        ),
        in_specs=[hbm] * 7,
        out_specs=(vmem, vmem),
        scratch_shapes=[
            pltpu.VMEM(images.shape, images.dtype),
            pltpu.VMEM((segs, 2, SHIFTS), jnp.int32),
            pltpu.VMEM((segs, SHIFTS), jnp.int32),
            pltpu.VMEM((1, segs), jnp.float32),
            pltpu.VMEM((1, segs), jnp.int32),
            pltpu.VMEM((1, 1), jnp.int32),
            pltpu.VMEM((128, 128), jnp.float32),
            pltpu.VMEM((segs, 128), jnp.float32),
            pltpu.VMEM((fils, 2, rows, kcols), jnp.bfloat16),
            pltpu.VMEM((fils, segs, 128), jnp.float32),
            pltpu.VMEM((fils, block, kcols), jnp.float32),
            pltpu.VMEM((fils, block, kcols), jnp.bfloat16),
            pltpu.VMEM((fils, block, kcols), jnp.bfloat16),
            pltpu.VMEM((segs * SHIFTS, fils * kcols), jnp.float32),
            pltpu.VMEM((segs * row_devs, 128), jnp.float32),
            pltpu.VMEM((row_devs, segs, 128), jnp.float32),
            pltpu.VMEM((row_devs, segs, 128), jnp.float32),
            dma((fils,)),
            dma((fils,)),
            dma((fils,)),
            dma((fils,)),
            dma((fils,)),
            dma((fils,)),
            dma((row_devs,)),
            dma((row_devs,)),
            dma((7,)),
        ],
        compiler_params=pltpu.CompilerParams(
            collective_id=0, has_side_effects=True, vmem_limit_bytes=32 * 1024 * 1024
        ),
    )(
        images,
        references[0],
        jnp.transpose(offsets, (0, 2, 1)),
        posterior,
        defocus[None],
        class_ids[None],
        seg_count[None],
    )
    return scores[:, : per * fils].reshape(segs, per, fils), averages


def fits(mesh):
    fils, row_devs = mesh.shape["fil"], mesh.shape["row"]
    return fils == 8 and FROWS == 8 * fils * row_devs and SHIFTS == 8 * row_devs


def solution(mesh):
    placed = (
        P("fil", None, "row", None),
        P("fil"),
        P("fil", None, "row", None),
        P("fil", None, None),
        P("fil", None),
        P("fil"),
        P("fil"),
    )
    return jax.shard_map(
        per_device_fused if fits(mesh) else per_device,
        mesh=mesh,
        in_specs=placed,
        out_specs=(P("fil", "row", None), P(None, ("row", "fil"))),
        check_vma=False,
    )
```

```python
import math

import jax
import jax.numpy as jnp
from jax import lax
from jax.experimental import pallas as pl
from jax.experimental.pallas import tpu as pltpu
from jax.sharding import PartitionSpec as P

MESH = pl.DeviceIdType.MESH

FROWS = 256
SHIFTS = 32
CLASSES = 16
SEG_FIL = 8


def wave_tables(shift_rows, shift_cols, row_freq, col_freq, box):
    row_angle = (shift_rows[..., None] * row_freq % box).astype(jnp.float32) * (
        -2.0 * math.pi / box
    )
    col_angle = (shift_cols[..., None] * col_freq % box).astype(jnp.float32) * (
        -2.0 * math.pi / box
    )
    row_cos = jnp.cos(row_angle)[..., :, None]
    row_sin = jnp.sin(row_angle)[..., :, None]
    col_cos = jnp.cos(col_angle)[..., None, :]
    col_sin = jnp.sin(col_angle)[..., None, :]
    phase_re = row_cos * col_cos - row_sin * col_sin
    phase_im = row_cos * col_sin + row_sin * col_cos
    return (phase_re, phase_im)


def contrast(defocus_vals, row_freq, col_freq, box):
    radius = (row_freq[:, None] * row_freq[:, None] + col_freq[None, :] * col_freq[None, :]).astype(
        jnp.float32
    ) / float(box * box)
    return -jnp.sin(200.0 * defocus_vals[:, None, None] * radius[None] + 0.1)


def aligned_rows(block_images, gain, block_offsets, row_freq, col_freq, box):
    phase_re, phase_im = wave_tables(
        block_offsets[..., 0], block_offsets[..., 1], row_freq, col_freq, box
    )
    scaled = gain[:, None]
    real_part = block_images[:, 0].astype(jnp.float32)[:, None]
    imag_part = block_images[:, 1].astype(jnp.float32)[:, None]
    aligned_re = scaled * (real_part * phase_re - imag_part * phase_im)
    aligned_im = scaled * (real_part * phase_im + imag_part * phase_re)
    stacked = jnp.stack([aligned_re, aligned_im], axis=3).astype(jnp.bfloat16)
    return stacked.reshape(stacked.shape[0] * stacked.shape[1], -1)


def correlate(aligned, panel):
    return lax.dot_general(
        aligned, panel, (((1,), (1,)), ((), ())), preferred_element_type=jnp.float32
    )


def per_device(images, defocus, references, offsets, posterior, class_ids, seg_count):
    seg_dev = images.shape[0]
    rows = images.shape[2]
    cols = images.shape[3]
    box = FROWS
    row_first = lax.axis_index("row") * rows
    row_freq = (row_first + jnp.arange(rows, dtype=jnp.int32) + box // 2) % box - box // 2
    col_freq = jnp.arange(cols, dtype=jnp.int32)
    live = (
        (jnp.arange(SEG_FIL, dtype=jnp.int32)[None, :] < seg_count[:, None])
        .reshape(-1)
        .astype(jnp.float32)
    )
    weight = live[:, None] * posterior.astype(jnp.float32) / 256.0
    local_panel = jnp.transpose(references, (0, 2, 1, 3)).reshape(references.shape[0], -1)
    classes = jnp.arange(CLASSES, dtype=jnp.int32)
    blocks = seg_dev // 8
    panel = lax.all_gather(local_panel, "fil", axis=0, tiled=True)

    def step(carry, inputs):
        numer, denom = carry
        block_images, block_defocus, block_offsets, block_weight, block_live, block_ids = inputs
        ctf = contrast(block_defocus, row_freq, col_freq, box)
        aligned = aligned_rows(
            block_images, ctf * block_live[:, None, None], block_offsets, row_freq, col_freq, box
        )
        block_scores = correlate(aligned, panel)
        member = (block_ids[None, :] == classes[:, None]).astype(jnp.float32)
        spread = (member[:, :, None] * block_weight[None]).astype(jnp.bfloat16).reshape(CLASSES, -1)
        numer = numer + jnp.dot(spread, aligned, preferred_element_type=jnp.float32)
        totals = member * jnp.sum(block_weight, axis=1)[None, :]
        denom = denom + jnp.dot(
            totals,
            (ctf * ctf).reshape(ctf.shape[0], -1),
            precision=lax.Precision.HIGHEST,
            preferred_element_type=jnp.float32,
        )
        return ((numer, denom), block_scores.reshape(8, SHIFTS, -1))

    inputs = (
        images.reshape(blocks, 8, 2, rows, cols),
        defocus.reshape(blocks, 8),
        offsets.reshape(blocks, 8, SHIFTS, 2),
        weight.reshape(blocks, 8, SHIFTS),
        live.reshape(blocks, 8),
        class_ids.reshape(blocks, 8),
    )
    start = (
        jnp.zeros((CLASSES, rows * 2 * cols), jnp.float32),
        jnp.zeros((CLASSES, rows * cols), jnp.float32),
    )
    (numer, denom), partial_scores = lax.scan(step, start, inputs)
    scores = lax.psum_scatter(
        partial_scores.reshape(seg_dev, SHIFTS, -1), "row", scatter_dimension=1, tiled=True
    )
    share = rows * 2 * cols // lax.axis_size("fil")
    total_numer, total_denom = lax.psum((numer, denom), "fil")
    wide = jnp.broadcast_to(
        total_denom.reshape(CLASSES, rows, 1, cols), (CLASSES, rows, 2, cols)
    ).reshape(CLASSES, -1)
    whole_avg = total_numer * lax.rsqrt(wide + 1.0)
    averages = lax.dynamic_slice_in_dim(whole_avg, lax.axis_index("fil") * share, share, 1)
    return (scores, averages)


SINE = (
    6.283185139080197,
    -41.34161488788259,
    81.60061435566797,
    -76.62117706362086,
    41.37130756865165,
    -12.514333309608835,
)
NEAREST = 12582912.0
DEFOCUS, TOTAL, LIVE = 16, 17, 18


def sine_turns(turns):
    r = turns - ((turns + NEAREST) - NEAREST)
    z = r * r
    p = jnp.full_like(z, SINE[-1])
    for c in SINE[-2::-1]:
        p = p * z + c
    return p * r


def floats(shape, axis):
    return lax.broadcasted_iota(jnp.int32, shape, axis).astype(jnp.float32)


def split(x):
    hi = x.astype(jnp.bfloat16)
    return hi, (x - hi.astype(jnp.float32)).astype(jnp.bfloat16)


def mm(a, b, contract_a=1):
    return lax.dot_general(
        a, b, (((contract_a,), (0,)), ((), ())), preferred_element_type=jnp.float32
    )


def ctf_of(defocus, kw, kx, box):
    radius = (kw * kw + kx * kx) * (1.0 / (box * box))
    arg = 200.0 * defocus * radius + 0.1
    return -sine_turns(arg * (0.5 / math.pi))


def fused(
    fils,
    row_devs,
    img_hbm,
    refs,
    offsets_hbm,
    posterior_hbm,
    defocus_hbm,
    ids_hbm,
    count_hbm,
    scores_out,
    avg_out,
    img,
    offsets,
    posterior,
    defocus_in,
    ids_in,
    count_in,
    turned,
    tile,
    refs_all,
    tiles_all,
    pf,
    pbuf,
    precv,
    fbuf,
    yscr,
    sbuf,
    srecv,
    ref_send,
    ref_recv,
    tile_send,
    tile_recv,
    p_send,
    p_recv,
    s_send,
    s_recv,
    in_sem,
):
    segs, _, rows, kcols = img.shape
    box = FROWS
    own = rows // fils
    fil = lax.axis_index("fil")
    row = lax.axis_index("row")

    def fil_peer(k):
        return lax.rem(fil + k, fils)

    def row_peer(k):
        return lax.rem(row + k, row_devs)

    barrier = pltpu.get_barrier_semaphore()
    for k in range(1, fils):
        pl.semaphore_signal(barrier, inc=1, device_id=(fil_peer(k), row), device_id_type=MESH)
    for k in range(1, row_devs):
        pl.semaphore_signal(barrier, inc=1, device_id=(fil, row_peer(k)), device_id_type=MESH)
    pulls = [
        pltpu.make_async_copy(src, dst, in_sem.at[j])
        for j, (src, dst) in enumerate(
            (
                (offsets_hbm, offsets),
                (posterior_hbm, posterior),
                (defocus_hbm, defocus_in),
                (ids_hbm, ids_in),
                (count_hbm, count_in),
                (img_hbm, img),
                (refs, refs_all.at[fil]),
            )
        )
    ]
    for c in pulls:
        c.start()

    def to_fil(k, src, dst_all, send, recv):
        return pltpu.make_async_remote_copy(
            src_ref=src,
            dst_ref=dst_all.at[fil],
            send_sem=send.at[k],
            recv_sem=recv.at[fil],
            device_id=(fil_peer(k), row),
            device_id_type=MESH,
        )

    def from_fil(k, dst_all, send, recv):
        d = fil_peer(k)
        return pltpu.make_async_remote_copy(
            src_ref=dst_all.at[d],
            dst_ref=dst_all.at[d],
            send_sem=send.at[k],
            recv_sem=recv.at[d],
            device_id=(d, row),
            device_id_type=MESH,
        )

    for c in pulls[:5]:
        c.wait()
    turned[...] = jnp.zeros_like(turned)
    shifts = offsets[...].astype(jnp.float32)
    turned[0:segs, 0:SHIFTS] = shifts[:, 0, :]
    turned[segs : 2 * segs, 0:SHIFTS] = shifts[:, 1, :]
    turned[2 * segs : 3 * segs, 0:SHIFTS] = posterior[...].astype(jnp.float32) * (1.0 / 256.0)
    turned[3 * segs : 3 * segs + 1, 0:segs] = ids_in[...].astype(jnp.float32)
    turned[3 * segs + 1 : 3 * segs + 2, 0:segs] = defocus_in[...]
    up = jnp.transpose(turned[...])
    weights = turned[2 * segs : 3 * segs, :]
    live = (floats((segs, 1), 0) < count_in[...].astype(jnp.float32)).astype(jnp.float32)
    sums = live * jnp.sum(weights, axis=1, keepdims=True)
    ids_col = up[0:segs, 3 * segs : 3 * segs + 1]
    def_col = up[0:segs, 3 * segs + 1 : 3 * segs + 2]
    at_lane = floats((segs, 128), 1)
    hot = jnp.where(ids_col == at_lane, 1.0, 0.0)
    tile[...] = jnp.where(
        at_lane == DEFOCUS,
        def_col,
        jnp.where(at_lane == TOTAL, sums, jnp.where(at_lane == LIVE, live, hot)),
    )
    tiles_all[fil] = tile[...]

    pairs = segs * SHIFTS

    def column(j):
        first = j * segs
        return jnp.concatenate(
            [up[0:SHIFTS, first + i : first + i + 1] for i in range(segs)], axis=0
        )

    sy, sx, wt = column(0), column(1), column(2)
    lane = lax.broadcasted_iota(jnp.int32, (1, 2 * rows), 1)
    ky = (row * rows + lax.rem(lane, rows)).astype(jnp.float32)
    kw = jnp.where(ky >= box // 2, ky - box, ky)
    low = lane < rows
    q = -(sy * kw)
    wave_a = sine_turns((q + jnp.where(low, 64.0, 128.0)) * (1.0 / box))
    kx = floats((1, kcols), 1)
    qc = -(sx * kx)
    col_cos = sine_turns((qc + 64.0) * (1.0 / box))
    col_sin = sine_turns(qc * (1.0 / box))

    pl.semaphore_wait(barrier, fils + row_devs - 2)
    partner = fil + 1 - 2 * lax.rem(fil, 2)
    ref_copies = []
    for k in range(fils // 2, 0, -1):
        d = fil_peer(2 * k) if 2 * k < fils else partner
        ref_copies.append(
            pltpu.make_async_remote_copy(
                src_ref=refs,
                dst_ref=refs_all.at[fil],
                send_sem=ref_send.at[k],
                recv_sem=ref_recv.at[fil],
                device_id=(d, row),
                device_id_type=MESH,
            )
        )
    for c in ref_copies:
        c.start()
    tile_copies = [to_fil(k, tile, tiles_all, tile_send, tile_recv) for k in range(1, fils)]
    for c in tile_copies:
        c.start()

    a_hi, a_lo = split(wave_a)
    c_hi, c_lo = split(jnp.concatenate([col_cos * wt, col_sin * wt], axis=1))

    kyl = (row * rows).astype(jnp.float32) + floats((rows, 1), 0)
    kwl = jnp.where(kyl >= box // 2, kyl - box, kyl)
    gains = []
    pulls[5].wait()
    for i in range(segs):
        ctf = ctf_of(tile[i : i + 1, DEFOCUS : DEFOCUS + 1], kwl, kx, box)
        g = ctf * tile[i : i + 1, LIVE : LIVE + 1]
        g_re = g * img[i, 0].astype(jnp.float32)
        g_im = g * img[i, 1].astype(jnp.float32)
        gains.append((g_re, g_im))
        at = slice(i * SHIFTS, (i + 1) * SHIFTS)
        grid = mm(
            jnp.concatenate([a_hi[at], a_hi[at], a_lo[at]], axis=0),
            jnp.concatenate([c_hi[at], c_lo[at], c_hi[at]], axis=0),
            contract_a=0,
        )
        w_re = grid[:rows, :kcols] + grid[rows:, kcols:]
        w_im = grid[:rows, kcols:] - grid[rows:, :kcols]
        p_re = g_re * w_re - g_im * w_im
        p_im = g_re * w_im + g_im * w_re
        for d in range(fils):
            part = slice(d * own, (d + 1) * own)
            pf[d, pl.ds(i, own, stride=2 * segs), :] = p_re[part]
            pf[d, pl.ds(segs + i, own, stride=2 * segs), :] = p_im[part]

    p_copies = []
    for k in sorted(range(1, fils), key=lambda k: abs(k - fils // 2)):
        d = fil_peer(k)
        pbuf[d] = pf[d].astype(jnp.bfloat16)
        c = to_fil(k, pbuf.at[d], precv, p_send, p_recv)
        c.start()
        p_copies.append(c)
    precv[fil] = pf[fil].astype(jnp.bfloat16)

    for k in range(2, fils, 2):
        from_fil(k, refs_all, ref_send, ref_recv).wait_recv()
        d = fil_peer(k)
        c = pltpu.make_async_remote_copy(
            src_ref=refs_all.at[d],
            dst_ref=refs_all.at[d],
            send_sem=ref_send.at[fils // 2 + k // 2],
            recv_sem=ref_recv.at[d],
            device_id=(partner, row),
            device_id_type=MESH,
        )
        c.start()
        ref_copies.append(c)

    for k in range(1, fils):
        from_fil(k, tiles_all, tile_send, tile_recv).wait_recv()
    every = fils * segs
    tiles = tiles_all[...].reshape(every, 128)
    member = jnp.transpose(tiles)[:CLASSES].astype(jnp.bfloat16)
    defocus = tiles[:, DEFOCUS : DEFOCUS + 1]
    total = tiles[:, TOTAL : TOTAL + 1]
    squares = []
    for y in range(own):
        k0 = (row * rows + fil * own + y).astype(jnp.float32)
        k0 = jnp.where(k0 >= box // 2, k0 - box, k0)
        ctf = ctf_of(defocus, k0, kx, box)
        squares.append(total * (ctf * ctf))
    d_hi, d_lo = split(jnp.concatenate(squares, axis=1))
    denom = mm(member, d_hi) + mm(member, d_lo)
    scale = lax.rsqrt(denom + 1.0)

    wave_b = sine_turns((q + jnp.where(low, 0.0, 64.0)) * (1.0 / box))
    b_hi, b_lo = split(wave_b)
    pulls[6].wait()
    for k in range(0, fils // 2):
        d = lax.rem(partner + 2 * k, fils)
        pltpu.make_async_remote_copy(
            src_ref=refs_all.at[d],
            dst_ref=refs_all.at[d],
            send_sem=ref_send.at[0],
            recv_sem=ref_recv.at[d],
            device_id=(partner, row),
            device_id_type=MESH,
        ).wait_recv()
    for i in range(segs):
        at = slice(i * SHIFTS, (i + 1) * SHIFTS)
        lhs = jnp.concatenate([a_hi[at], b_hi[at], a_lo[at], b_lo[at]], axis=0)
        g_re, g_im = gains[i]
        for r in range(0, fils, 2):
            panel = []
            for e in (r, r + 1):
                f_re = refs_all[e, 0].astype(jnp.float32)
                f_im = refs_all[e, 1].astype(jnp.float32)
                q_re = g_re * f_re + g_im * f_im
                q_im = g_im * f_re - g_re * f_im
                panel.append(jnp.concatenate([q_re, q_im], axis=0).astype(jnp.bfloat16))
            z = mm(lhs, jnp.concatenate(panel, axis=1))
            z = z[: 2 * SHIFTS] + z[2 * SHIFTS :]
            for e in (0, 1):
                ze = z[:, e * kcols : (e + 1) * kcols]
                fbuf[at, (r + e) * kcols : (r + e + 1) * kcols] = (
                    col_cos[at] * ze[:SHIFTS] - col_sin[at] * ze[SHIFTS:]
                )
    f_hi, f_lo = split(fbuf[...])
    lane = lax.broadcasted_iota(jnp.int32, (1, 128), 1)
    ones = jnp.concatenate(
        [
            jnp.broadcast_to((lane & (fils - 1) == r).astype(jnp.float32), (kcols, 128))
            for r in range(fils)
        ],
        axis=0,
    ).astype(jnp.bfloat16)
    spread = mm(f_hi, ones) + mm(f_lo, ones)
    per = SHIFTS // row_devs
    pick = (
        lax.broadcasted_iota(jnp.int32, (per, 128), 1) // fils
        == lax.broadcasted_iota(jnp.int32, (per, 128), 0)
    ).astype(jnp.float32)
    yscr[...] = jnp.sum(spread.reshape(pairs // per, per, 128) * pick[None], axis=1)
    for j in range(row_devs):
        sbuf[j] = yscr[pl.ds(j, segs, stride=row_devs), :]
    s_copies = []
    for k in range(1, row_devs):
        c = pltpu.make_async_remote_copy(
            src_ref=sbuf.at[row_peer(k)],
            dst_ref=srecv.at[row],
            send_sem=s_send.at[k],
            recv_sem=s_recv.at[row],
            device_id=(fil, row_peer(k)),
            device_id_type=MESH,
        )
        c.start()
        s_copies.append(c)

    for k in range(1, fils):
        from_fil(k, precv, p_send, p_recv).wait_recv()
    parts = precv[...].astype(jnp.float32).reshape(fils, 2 * own, segs, kcols)
    for y in range(own):
        for part in range(2):
            t = 2 * y + part
            rhs = parts[:, t].reshape(every, kcols).astype(jnp.bfloat16)
            avg_out[:, t * kcols : (t + 1) * kcols] = (
                mm(member, rhs) * scale[:, y * kcols : (y + 1) * kcols]
            )

    acc = sbuf[row]
    for k in range(1, row_devs):
        q = row_peer(k)
        pltpu.make_async_remote_copy(
            src_ref=srecv.at[q],
            dst_ref=srecv.at[q],
            send_sem=s_send.at[k],
            recv_sem=s_recv.at[q],
            device_id=(fil, q),
            device_id_type=MESH,
        ).wait_recv()
        acc = acc + srecv[q]
    for j in range(per):
        scores_out[:, j, :] = acc[:, j * fils : (j + 1) * fils]
    for c in tile_copies + ref_copies + p_copies + s_copies:
        c.wait_send()


def hand_over(scores, averages, scores_out, avg_out, sem):
    first = pltpu.make_async_copy(averages, avg_out, sem.at[0])
    second = pltpu.make_async_copy(scores, scores_out, sem.at[1])
    first.start()
    second.start()
    first.wait()
    second.wait()


def per_device_fused(images, defocus, references, offsets, posterior, class_ids, seg_count):
    segs, _, rows, kcols = images.shape
    fils = lax.axis_size("fil")
    row_devs = lax.axis_size("row")
    own = rows // fils
    block = 2 * own * segs
    per = SHIFTS // row_devs
    vmem = pl.BlockSpec(memory_space=pltpu.VMEM)
    hbm = pl.BlockSpec(memory_space=pl.ANY)
    dma = pltpu.SemaphoreType.DMA

    def kernel(*refs):
        fused(fils, row_devs, *refs)

    scores, averages = pl.pallas_call(
        kernel,
        out_shape=(
            jax.ShapeDtypeStruct((segs, per, fils), jnp.float32),
            jax.ShapeDtypeStruct((CLASSES, 2 * own * kcols), jnp.float32),
        ),
        in_specs=[hbm] * 7,
        out_specs=(vmem, vmem),
        scratch_shapes=[
            pltpu.VMEM(images.shape, images.dtype),
            pltpu.VMEM((segs, 2, SHIFTS), jnp.int32),
            pltpu.VMEM((segs, SHIFTS), jnp.int32),
            pltpu.VMEM((1, segs), jnp.float32),
            pltpu.VMEM((1, segs), jnp.int32),
            pltpu.VMEM((1, 1), jnp.int32),
            pltpu.VMEM((128, 128), jnp.float32),
            pltpu.VMEM((segs, 128), jnp.float32),
            pltpu.VMEM((fils, 2, rows, kcols), jnp.bfloat16),
            pltpu.VMEM((fils, segs, 128), jnp.float32),
            pltpu.VMEM((fils, block, kcols), jnp.float32),
            pltpu.VMEM((fils, block, kcols), jnp.bfloat16),
            pltpu.VMEM((fils, block, kcols), jnp.bfloat16),
            pltpu.VMEM((segs * SHIFTS, fils * kcols), jnp.float32),
            pltpu.VMEM((segs * row_devs, 128), jnp.float32),
            pltpu.VMEM((row_devs, segs, 128), jnp.float32),
            pltpu.VMEM((row_devs, segs, 128), jnp.float32),
            dma((fils,)),
            dma((fils,)),
            dma((fils,)),
            dma((fils,)),
            dma((fils,)),
            dma((fils,)),
            dma((row_devs,)),
            dma((row_devs,)),
            dma((7,)),
        ],
        compiler_params=pltpu.CompilerParams(
            collective_id=0, has_side_effects=True, vmem_limit_bytes=60 * 1024 * 1024
        ),
    )(
        images,
        references[0],
        jnp.transpose(offsets, (0, 2, 1)),
        posterior,
        defocus[None],
        class_ids[None],
        seg_count[None],
    )
    return pl.pallas_call(
        hand_over,
        out_shape=(
            jax.ShapeDtypeStruct(scores.shape, scores.dtype),
            jax.ShapeDtypeStruct(averages.shape, averages.dtype),
        ),
        in_specs=[hbm] * 2,
        out_specs=(hbm, hbm),
        scratch_shapes=[dma((2,))],
        compiler_params=pltpu.CompilerParams(vmem_limit_bytes=60 * 1024 * 1024),
    )(scores, averages)


def fits(mesh):
    fils, row_devs = mesh.shape["fil"], mesh.shape["row"]
    return fils == 8 and FROWS == 8 * fils * row_devs and SHIFTS == 8 * row_devs


def solution(mesh):
    placed = (
        P("fil", None, "row", None),
        P("fil"),
        P("fil", None, "row", None),
        P("fil", None, None),
        P("fil", None),
        P("fil"),
        P("fil"),
    )
    return jax.shard_map(
        per_device_fused if fits(mesh) else per_device,
        mesh=mesh,
        in_specs=placed,
        out_specs=(P("fil", "row", None), P(None, ("row", "fil"))),
        check_vma=False,
    )
```

```python
import math

import jax
import jax.numpy as jnp
from jax import lax
from jax.experimental import pallas as pl
from jax.experimental.pallas import tpu as pltpu
from jax.sharding import PartitionSpec as P

MESH = pl.DeviceIdType.MESH

FROWS = 256
SHIFTS = 32
CLASSES = 16
SEG_FIL = 8


def wave_tables(shift_rows, shift_cols, row_freq, col_freq, box):
    row_angle = (shift_rows[..., None] * row_freq % box).astype(jnp.float32) * (
        -2.0 * math.pi / box
    )
    col_angle = (shift_cols[..., None] * col_freq % box).astype(jnp.float32) * (
        -2.0 * math.pi / box
    )
    row_cos = jnp.cos(row_angle)[..., :, None]
    row_sin = jnp.sin(row_angle)[..., :, None]
    col_cos = jnp.cos(col_angle)[..., None, :]
    col_sin = jnp.sin(col_angle)[..., None, :]
    phase_re = row_cos * col_cos - row_sin * col_sin
    phase_im = row_cos * col_sin + row_sin * col_cos
    return (phase_re, phase_im)


def contrast(defocus_vals, row_freq, col_freq, box):
    radius = (row_freq[:, None] * row_freq[:, None] + col_freq[None, :] * col_freq[None, :]).astype(
        jnp.float32
    ) / float(box * box)
    return -jnp.sin(200.0 * defocus_vals[:, None, None] * radius[None] + 0.1)


def aligned_rows(block_images, gain, block_offsets, row_freq, col_freq, box):
    phase_re, phase_im = wave_tables(
        block_offsets[..., 0], block_offsets[..., 1], row_freq, col_freq, box
    )
    scaled = gain[:, None]
    real_part = block_images[:, 0].astype(jnp.float32)[:, None]
    imag_part = block_images[:, 1].astype(jnp.float32)[:, None]
    aligned_re = scaled * (real_part * phase_re - imag_part * phase_im)
    aligned_im = scaled * (real_part * phase_im + imag_part * phase_re)
    stacked = jnp.stack([aligned_re, aligned_im], axis=3).astype(jnp.bfloat16)
    return stacked.reshape(stacked.shape[0] * stacked.shape[1], -1)


def correlate(aligned, panel):
    return lax.dot_general(
        aligned, panel, (((1,), (1,)), ((), ())), preferred_element_type=jnp.float32
    )


def per_device(images, defocus, references, offsets, posterior, class_ids, seg_count):
    seg_dev = images.shape[0]
    rows = images.shape[2]
    cols = images.shape[3]
    box = FROWS
    row_first = lax.axis_index("row") * rows
    row_freq = (row_first + jnp.arange(rows, dtype=jnp.int32) + box // 2) % box - box // 2
    col_freq = jnp.arange(cols, dtype=jnp.int32)
    live = (
        (jnp.arange(SEG_FIL, dtype=jnp.int32)[None, :] < seg_count[:, None])
        .reshape(-1)
        .astype(jnp.float32)
    )
    weight = live[:, None] * posterior.astype(jnp.float32) / 256.0
    local_panel = jnp.transpose(references, (0, 2, 1, 3)).reshape(references.shape[0], -1)
    classes = jnp.arange(CLASSES, dtype=jnp.int32)
    blocks = seg_dev // 8
    panel = lax.all_gather(local_panel, "fil", axis=0, tiled=True)

    def step(carry, inputs):
        numer, denom = carry
        block_images, block_defocus, block_offsets, block_weight, block_live, block_ids = inputs
        ctf = contrast(block_defocus, row_freq, col_freq, box)
        aligned = aligned_rows(
            block_images, ctf * block_live[:, None, None], block_offsets, row_freq, col_freq, box
        )
        block_scores = correlate(aligned, panel)
        member = (block_ids[None, :] == classes[:, None]).astype(jnp.float32)
        spread = (member[:, :, None] * block_weight[None]).astype(jnp.bfloat16).reshape(CLASSES, -1)
        numer = numer + jnp.dot(spread, aligned, preferred_element_type=jnp.float32)
        totals = member * jnp.sum(block_weight, axis=1)[None, :]
        denom = denom + jnp.dot(
            totals,
            (ctf * ctf).reshape(ctf.shape[0], -1),
            precision=lax.Precision.HIGHEST,
            preferred_element_type=jnp.float32,
        )
        return ((numer, denom), block_scores.reshape(8, SHIFTS, -1))

    inputs = (
        images.reshape(blocks, 8, 2, rows, cols),
        defocus.reshape(blocks, 8),
        offsets.reshape(blocks, 8, SHIFTS, 2),
        weight.reshape(blocks, 8, SHIFTS),
        live.reshape(blocks, 8),
        class_ids.reshape(blocks, 8),
    )
    start = (
        jnp.zeros((CLASSES, rows * 2 * cols), jnp.float32),
        jnp.zeros((CLASSES, rows * cols), jnp.float32),
    )
    (numer, denom), partial_scores = lax.scan(step, start, inputs)
    scores = lax.psum_scatter(
        partial_scores.reshape(seg_dev, SHIFTS, -1), "row", scatter_dimension=1, tiled=True
    )
    share = rows * 2 * cols // lax.axis_size("fil")
    total_numer, total_denom = lax.psum((numer, denom), "fil")
    wide = jnp.broadcast_to(
        total_denom.reshape(CLASSES, rows, 1, cols), (CLASSES, rows, 2, cols)
    ).reshape(CLASSES, -1)
    whole_avg = total_numer * lax.rsqrt(wide + 1.0)
    averages = lax.dynamic_slice_in_dim(whole_avg, lax.axis_index("fil") * share, share, 1)
    return (scores, averages)


SINE = (
    6.283185139080197,
    -41.34161488788259,
    81.60061435566797,
    -76.62117706362086,
    41.37130756865165,
    -12.514333309608835,
)
NEAREST = 12582912.0
DEFOCUS, TOTAL, LIVE = 16, 17, 18


def sine_turns(turns):
    r = turns - ((turns + NEAREST) - NEAREST)
    z = r * r
    p = jnp.full_like(z, SINE[-1])
    for c in SINE[-2::-1]:
        p = p * z + c
    return p * r


def floats(shape, axis):
    return lax.broadcasted_iota(jnp.int32, shape, axis).astype(jnp.float32)


def split(x):
    hi = x.astype(jnp.bfloat16)
    return hi, (x - hi.astype(jnp.float32)).astype(jnp.bfloat16)


def mm(a, b, contract_a=1):
    return lax.dot_general(
        a, b, (((contract_a,), (0,)), ((), ())), preferred_element_type=jnp.float32
    )


def ctf_of(defocus, kw, kx, box):
    radius = (kw * kw + kx * kx) * (1.0 / (box * box))
    arg = 200.0 * defocus * radius + 0.1
    return -sine_turns(arg * (0.5 / math.pi))


def fused(
    fils,
    row_devs,
    img_hbm,
    refs,
    offsets_hbm,
    posterior_hbm,
    defocus_hbm,
    ids_hbm,
    count_hbm,
    scores_out,
    avg_out,
    img,
    offsets,
    posterior,
    defocus_in,
    ids_in,
    count_in,
    turned,
    tile,
    refs_all,
    tiles_all,
    pf,
    pbuf,
    precv,
    fbuf,
    yscr,
    sbuf,
    srecv,
    ref_send,
    ref_recv,
    tile_send,
    tile_recv,
    p_send,
    p_recv,
    s_send,
    s_recv,
    in_sem,
):
    segs, _, rows, kcols = img.shape
    box = FROWS
    own = rows // fils
    fil = lax.axis_index("fil")
    row = lax.axis_index("row")

    def fil_peer(k):
        return lax.rem(fil + k, fils)

    def row_peer(k):
        return lax.rem(row + k, row_devs)

    barrier = pltpu.get_barrier_semaphore()
    for k in range(1, fils):
        pl.semaphore_signal(barrier, inc=1, device_id=(fil_peer(k), row), device_id_type=MESH)
    for k in range(1, row_devs):
        pl.semaphore_signal(barrier, inc=1, device_id=(fil, row_peer(k)), device_id_type=MESH)
    pulls = [
        pltpu.make_async_copy(src, dst, in_sem.at[j])
        for j, (src, dst) in enumerate(
            (
                (offsets_hbm, offsets),
                (posterior_hbm, posterior),
                (defocus_hbm, defocus_in),
                (ids_hbm, ids_in),
                (count_hbm, count_in),
                (img_hbm, img),
                (refs, refs_all.at[fil]),
            )
        )
    ]
    for c in pulls:
        c.start()

    def to_fil(k, src, dst_all, send, recv):
        return pltpu.make_async_remote_copy(
            src_ref=src,
            dst_ref=dst_all.at[fil],
            send_sem=send.at[k],
            recv_sem=recv.at[fil],
            device_id=(fil_peer(k), row),
            device_id_type=MESH,
        )

    def from_fil(k, dst_all, send, recv):
        d = fil_peer(k)
        return pltpu.make_async_remote_copy(
            src_ref=dst_all.at[d],
            dst_ref=dst_all.at[d],
            send_sem=send.at[k],
            recv_sem=recv.at[d],
            device_id=(d, row),
            device_id_type=MESH,
        )

    for c in pulls[:5]:
        c.wait()
    turned[...] = jnp.zeros_like(turned)
    shifts = offsets[...].astype(jnp.float32)
    turned[0:segs, 0:SHIFTS] = shifts[:, 0, :]
    turned[segs : 2 * segs, 0:SHIFTS] = shifts[:, 1, :]
    turned[2 * segs : 3 * segs, 0:SHIFTS] = posterior[...].astype(jnp.float32) * (1.0 / 256.0)
    turned[3 * segs : 3 * segs + 1, 0:segs] = ids_in[...].astype(jnp.float32)
    turned[3 * segs + 1 : 3 * segs + 2, 0:segs] = defocus_in[...]
    up = jnp.transpose(turned[...])
    weights = turned[2 * segs : 3 * segs, :]
    live = (floats((segs, 1), 0) < count_in[...].astype(jnp.float32)).astype(jnp.float32)
    sums = live * jnp.sum(weights, axis=1, keepdims=True)
    ids_col = up[0:segs, 3 * segs : 3 * segs + 1]
    def_col = up[0:segs, 3 * segs + 1 : 3 * segs + 2]
    at_lane = floats((segs, 128), 1)
    hot = jnp.where(ids_col == at_lane, 1.0, 0.0)
    tile[...] = jnp.where(
        at_lane == DEFOCUS,
        def_col,
        jnp.where(at_lane == TOTAL, sums, jnp.where(at_lane == LIVE, live, hot)),
    )
    tiles_all[fil] = tile[...]

    pairs = segs * SHIFTS

    def column(j):
        first = j * segs
        return jnp.concatenate(
            [up[0:SHIFTS, first + i : first + i + 1] for i in range(segs)], axis=0
        )

    sy, sx, wt = column(0), column(1), column(2)
    lane = lax.broadcasted_iota(jnp.int32, (1, 2 * rows), 1)
    ky = (row * rows + lax.rem(lane, rows)).astype(jnp.float32)
    kw = jnp.where(ky >= box // 2, ky - box, ky)
    low = lane < rows
    q = -(sy * kw)
    wave_a = sine_turns((q + jnp.where(low, 64.0, 128.0)) * (1.0 / box))
    kx = floats((1, kcols), 1)
    qc = -(sx * kx)
    col_cos = sine_turns((qc + 64.0) * (1.0 / box))
    col_sin = sine_turns(qc * (1.0 / box))

    pl.semaphore_wait(barrier, fils + row_devs - 2)
    partner = fil + 1 - 2 * lax.rem(fil, 2)
    ref_copies = []
    for k in range(fils // 2, 0, -1):
        d = fil_peer(2 * k) if 2 * k < fils else partner
        ref_copies.append(
            pltpu.make_async_remote_copy(
                src_ref=refs,
                dst_ref=refs_all.at[fil],
                send_sem=ref_send.at[k],
                recv_sem=ref_recv.at[fil],
                device_id=(d, row),
                device_id_type=MESH,
            )
        )
    for c in ref_copies:
        c.start()
    tile_copies = [to_fil(k, tile, tiles_all, tile_send, tile_recv) for k in range(1, fils)]
    for c in tile_copies:
        c.start()

    a_hi, a_lo = split(wave_a)
    c_hi, c_lo = split(jnp.concatenate([col_cos * wt, col_sin * wt], axis=1))

    kyl = (row * rows).astype(jnp.float32) + floats((rows, 1), 0)
    kwl = jnp.where(kyl >= box // 2, kyl - box, kyl)
    gains = []
    pulls[5].wait()
    for i in range(segs):
        ctf = ctf_of(tile[i : i + 1, DEFOCUS : DEFOCUS + 1], kwl, kx, box)
        g = ctf * tile[i : i + 1, LIVE : LIVE + 1]
        g_re = g * img[i, 0].astype(jnp.float32)
        g_im = g * img[i, 1].astype(jnp.float32)
        gains.append((g_re, g_im))
        at = slice(i * SHIFTS, (i + 1) * SHIFTS)
        grid = mm(
            jnp.concatenate([a_hi[at], a_hi[at], a_lo[at]], axis=0),
            jnp.concatenate([c_hi[at], c_lo[at], c_hi[at]], axis=0),
            contract_a=0,
        )
        w_re = grid[:rows, :kcols] + grid[rows:, kcols:]
        w_im = grid[:rows, kcols:] - grid[rows:, :kcols]
        p_re = g_re * w_re - g_im * w_im
        p_im = g_re * w_im + g_im * w_re
        for d in range(fils):
            part = slice(d * own, (d + 1) * own)
            pf[d, pl.ds(i, own, stride=2 * segs), :] = p_re[part]
            pf[d, pl.ds(segs + i, own, stride=2 * segs), :] = p_im[part]

    p_copies = []
    for k in sorted(range(1, fils), key=lambda k: abs(k - fils // 2)):
        d = fil_peer(k)
        pbuf[d] = pf[d].astype(jnp.bfloat16)
        c = to_fil(k, pbuf.at[d], precv, p_send, p_recv)
        c.start()
        p_copies.append(c)
    precv[fil] = pf[fil].astype(jnp.bfloat16)

    for k in range(2, fils, 2):
        from_fil(k, refs_all, ref_send, ref_recv).wait_recv()
        d = fil_peer(k)
        c = pltpu.make_async_remote_copy(
            src_ref=refs_all.at[d],
            dst_ref=refs_all.at[d],
            send_sem=ref_send.at[fils // 2 + k // 2],
            recv_sem=ref_recv.at[d],
            device_id=(partner, row),
            device_id_type=MESH,
        )
        c.start()
        ref_copies.append(c)

    for k in range(1, fils):
        from_fil(k, tiles_all, tile_send, tile_recv).wait_recv()
    every = fils * segs
    tiles = tiles_all[...].reshape(every, 128)
    member = jnp.transpose(tiles)[:CLASSES].astype(jnp.bfloat16)
    defocus = tiles[:, DEFOCUS : DEFOCUS + 1]
    total = tiles[:, TOTAL : TOTAL + 1]
    squares = []
    for y in range(own):
        k0 = (row * rows + fil * own + y).astype(jnp.float32)
        k0 = jnp.where(k0 >= box // 2, k0 - box, k0)
        ctf = ctf_of(defocus, k0, kx, box)
        squares.append(total * (ctf * ctf))
    d_hi, d_lo = split(jnp.concatenate(squares, axis=1))
    denom = mm(member, d_hi) + mm(member, d_lo)
    scale = lax.rsqrt(denom + 1.0)

    wave_b = sine_turns((q + jnp.where(low, 0.0, 64.0)) * (1.0 / box))
    b_hi, b_lo = split(wave_b)
    pulls[6].wait()
    for k in range(0, fils // 2):
        d = lax.rem(partner + 2 * k, fils)
        pltpu.make_async_remote_copy(
            src_ref=refs_all.at[d],
            dst_ref=refs_all.at[d],
            send_sem=ref_send.at[0],
            recv_sem=ref_recv.at[d],
            device_id=(partner, row),
            device_id_type=MESH,
        ).wait_recv()
    for i in range(segs):
        at = slice(i * SHIFTS, (i + 1) * SHIFTS)
        lhs = jnp.concatenate([a_hi[at], b_hi[at], a_lo[at], b_lo[at]], axis=0)
        g_re, g_im = gains[i]
        for r in range(0, fils, 2):
            panel = []
            for e in (r, r + 1):
                f_re = refs_all[e, 0].astype(jnp.float32)
                f_im = refs_all[e, 1].astype(jnp.float32)
                q_re = g_re * f_re + g_im * f_im
                q_im = g_im * f_re - g_re * f_im
                panel.append(jnp.concatenate([q_re, q_im], axis=0).astype(jnp.bfloat16))
            z = mm(lhs, jnp.concatenate(panel, axis=1))
            z = z[: 2 * SHIFTS] + z[2 * SHIFTS :]
            for e in (0, 1):
                ze = z[:, e * kcols : (e + 1) * kcols]
                fbuf[at, (r + e) * kcols : (r + e + 1) * kcols] = (
                    col_cos[at] * ze[:SHIFTS] - col_sin[at] * ze[SHIFTS:]
                )
    f_hi, f_lo = split(fbuf[...])
    lane = lax.broadcasted_iota(jnp.int32, (1, 128), 1)
    ones = jnp.concatenate(
        [
            jnp.broadcast_to((lane & (fils - 1) == r).astype(jnp.float32), (kcols, 128))
            for r in range(fils)
        ],
        axis=0,
    ).astype(jnp.bfloat16)
    spread = mm(f_hi, ones) + mm(f_lo, ones)
    per = SHIFTS // row_devs
    pick = (
        lax.broadcasted_iota(jnp.int32, (per, 128), 1) // fils
        == lax.broadcasted_iota(jnp.int32, (per, 128), 0)
    ).astype(jnp.float32)
    yscr[...] = jnp.sum(spread.reshape(pairs // per, per, 128) * pick[None], axis=1)
    for j in range(row_devs):
        sbuf[j] = yscr[pl.ds(j, segs, stride=row_devs), :]
    s_copies = []
    for k in range(1, row_devs):
        c = pltpu.make_async_remote_copy(
            src_ref=sbuf.at[row_peer(k)],
            dst_ref=srecv.at[row],
            send_sem=s_send.at[k],
            recv_sem=s_recv.at[row],
            device_id=(fil, row_peer(k)),
            device_id_type=MESH,
        )
        c.start()
        s_copies.append(c)

    for k in range(1, fils):
        from_fil(k, precv, p_send, p_recv).wait_recv()
    parts = precv[...].astype(jnp.float32).reshape(fils, 2 * own, segs, kcols)
    for y in range(own):
        for part in range(2):
            t = 2 * y + part
            rhs = parts[:, t].reshape(every, kcols).astype(jnp.bfloat16)
            avg_out[:, t * kcols : (t + 1) * kcols] = (
                mm(member, rhs) * scale[:, y * kcols : (y + 1) * kcols]
            )

    acc = sbuf[row]
    for k in range(1, row_devs):
        q = row_peer(k)
        pltpu.make_async_remote_copy(
            src_ref=srecv.at[q],
            dst_ref=srecv.at[q],
            send_sem=s_send.at[k],
            recv_sem=s_recv.at[q],
            device_id=(fil, q),
            device_id_type=MESH,
        ).wait_recv()
        acc = acc + srecv[q]
    for j in range(per):
        scores_out[:, j, :] = acc[:, j * fils : (j + 1) * fils]
    for c in tile_copies + ref_copies + p_copies + s_copies:
        c.wait_send()


def hand_over(scores, averages, scores_out, avg_out):
    scores_out[...] = scores[...]
    avg_out[...] = averages[...]


def per_device_fused(images, defocus, references, offsets, posterior, class_ids, seg_count):
    segs, _, rows, kcols = images.shape
    fils = lax.axis_size("fil")
    row_devs = lax.axis_size("row")
    own = rows // fils
    block = 2 * own * segs
    per = SHIFTS // row_devs
    vmem = pl.BlockSpec(memory_space=pltpu.VMEM)
    hbm = pl.BlockSpec(memory_space=pl.ANY)
    dma = pltpu.SemaphoreType.DMA

    def kernel(*refs):
        fused(fils, row_devs, *refs)

    scores, averages = pl.pallas_call(
        kernel,
        out_shape=(
            jax.ShapeDtypeStruct((segs, per, fils), jnp.float32),
            jax.ShapeDtypeStruct((CLASSES, 2 * own * kcols), jnp.float32),
        ),
        in_specs=[hbm] * 7,
        out_specs=(vmem, vmem),
        scratch_shapes=[
            pltpu.VMEM(images.shape, images.dtype),
            pltpu.VMEM((segs, 2, SHIFTS), jnp.int32),
            pltpu.VMEM((segs, SHIFTS), jnp.int32),
            pltpu.VMEM((1, segs), jnp.float32),
            pltpu.VMEM((1, segs), jnp.int32),
            pltpu.VMEM((1, 1), jnp.int32),
            pltpu.VMEM((128, 128), jnp.float32),
            pltpu.VMEM((segs, 128), jnp.float32),
            pltpu.VMEM((fils, 2, rows, kcols), jnp.bfloat16),
            pltpu.VMEM((fils, segs, 128), jnp.float32),
            pltpu.VMEM((fils, block, kcols), jnp.float32),
            pltpu.VMEM((fils, block, kcols), jnp.bfloat16),
            pltpu.VMEM((fils, block, kcols), jnp.bfloat16),
            pltpu.VMEM((segs * SHIFTS, fils * kcols), jnp.float32),
            pltpu.VMEM((segs * row_devs, 128), jnp.float32),
            pltpu.VMEM((row_devs, segs, 128), jnp.float32),
            pltpu.VMEM((row_devs, segs, 128), jnp.float32),
            dma((fils,)),
            dma((fils,)),
            dma((fils,)),
            dma((fils,)),
            dma((fils,)),
            dma((fils,)),
            dma((row_devs,)),
            dma((row_devs,)),
            dma((7,)),
        ],
        compiler_params=pltpu.CompilerParams(
            collective_id=0, has_side_effects=True, vmem_limit_bytes=60 * 1024 * 1024
        ),
    )(
        images,
        references[0],
        jnp.transpose(offsets, (0, 2, 1)),
        posterior,
        defocus[None],
        class_ids[None],
        seg_count[None],
    )
    return pl.pallas_call(
        hand_over,
        out_shape=(
            jax.ShapeDtypeStruct(scores.shape, scores.dtype),
            jax.ShapeDtypeStruct(averages.shape, averages.dtype),
        ),
        in_specs=[vmem] * 2,
        out_specs=(vmem, vmem),
        compiler_params=pltpu.CompilerParams(vmem_limit_bytes=60 * 1024 * 1024),
    )(scores, averages)


def fits(mesh):
    fils, row_devs = mesh.shape["fil"], mesh.shape["row"]
    return fils == 8 and FROWS == 8 * fils * row_devs and SHIFTS == 8 * row_devs


def solution(mesh):
    placed = (
        P("fil", None, "row", None),
        P("fil"),
        P("fil", None, "row", None),
        P("fil", None, None),
        P("fil", None),
        P("fil"),
        P("fil"),
    )
    return jax.shard_map(
        per_device_fused if fits(mesh) else per_device,
        mesh=mesh,
        in_specs=placed,
        out_specs=(P("fil", "row", None), P(None, ("row", "fil"))),
        check_vma=False,
    )
```
